32 devices in a mesh: groups: 2 (over y), seq: 4 (over z), head: 2 (over x), sub: 2 (over core).
Axes of the slice: x: 2, y: 2, z: 4, core: 2. Of those that a mesh axis runs over, the one named last changes fastest.
Arguments:
- x_raw: bfloat16 [16, 128, 8192], P(('groups', 'seq', 'sub'), 'head'), parts along dimension 0, may hold values from -6 to 6
- bc_raw: bfloat16 [16, 128, 2048], P(('groups', 'seq', 'sub'), 'head'), parts along dimension 0, may hold values from -6 to 6
- dt_raw: bfloat16 [16, 128, 128], P(('groups', 'seq', 'sub'), 'head'), parts along dimension 0, may hold values from -3 to 40
- conv_x_weight: float32 [4, 8192], P(None, 'head'), may hold values from -3 to 3
- conv_x_bias: float32 [8192], P('head'), may hold values from -2.5 to 2.5
- conv_bc_weight: float32 [4, 2048], P(None, 'head'), may hold values from -3 to 3
- conv_bc_bias: float32 [2048], P('head'), may hold values from -2.5 to 2.5
- stride_offset_per_head: float32 [128], P('head'), may hold values from -12 to 0
- a_log: float32 [128], P('head'), may hold values from -8 to 3
- skip_d: float32 [128], P('head'), may hold values from 0.5 to 1.5
- norm_gain: float32 [8192], P('head'), may hold values from 0.1 to 1.9
Outputs:
- mixed: bfloat16 [16, 128, 8192], P(('groups', 'seq', 'sub'), None, 'head'), parts along dimension 0
The draws below stay inside these ranges and needn't reach their ends.
There are 2 independent parts, one for each index of `groups`. The reference program is written for one: setup_inputs(seed, part) draws one part's arguments, and reference() takes and returns one part's arrays. A program takes and returns all parts, laid end to end along the dimension named above; an argument that names none is the same for every part. Nothing has to cross between parts.
All inputs are finite; a program needn't handle non-finite values.
Results may differ from the reference program's by a relative error of at most 0.0061.
Values may be sent and summed in bfloat16 or wider, within the bound.
A program may use at most 128 MiB of HBM per device.

```python
import math
import jax
import jax.numpy as jnp
from jax import lax

HEADS = 128
HEAD_DIM = 64
STATE = 128
GROUPS = 8
CONV = 4
SPAN = 128
ROWS = 128
NBLOCKS = 8
SPELL_LENGTH = 1024
INNER = 8192


def head_table(key):
    seed_sequence = jax.random.split(jax.random.fold_in(key, 11), 4)
    fast_count = HEADS // 2
    order = jax.random.permutation(seed_sequence[0], HEADS)
    is_fast = order < fast_count
    slow_rate = jax.random.uniform(seed_sequence[1], (HEADS,), jnp.float32, 0.25, 0.45) * math.log(10.0) / SPELL_LENGTH
    fast_rate = 1.0 / jax.random.uniform(seed_sequence[2], (HEADS,), jnp.float32, 30.0, 50.0)
    decay_rate = jnp.where(is_fast, fast_rate, slow_rate)
    stored_values = jnp.minimum(1.0 / decay_rate, float(SPELL_LENGTH))
    spread = jnp.exp(jax.random.uniform(seed_sequence[3], (HEADS,), jnp.float32, -0.35, 0.35))
    step_size = spread / jnp.sqrt(STATE * stored_values)
    return (jnp.log(decay_rate / step_size), jnp.log(jnp.expm1(step_size)))


def draw_a_log(key, part):
    return head_table(key)[0]


def draw_stride_offset_per_head(key, part):
    return head_table(key)[1]


def draw_dt_raw(key, part):
    seed_sequence = jax.random.split(jax.random.fold_in(key, 23), 3)
    jitter = jax.random.uniform(seed_sequence[0], (NBLOCKS, ROWS, HEADS), jnp.float32, -0.7, 0.7)
    displacement = jax.random.uniform(seed_sequence[1], (NBLOCKS, 1, 1), jnp.float32, -0.5, 0.5)
    spell_index = jax.random.randint(seed_sequence[2], (3,), 0, SPELL_LENGTH)
    sequence_place = jnp.arange(NBLOCKS)[:, None] * ROWS + jnp.arange(ROWS)[None, :]
    marked_indicator = jnp.any(sequence_place[:, :, None] == spell_index[None, None, :], axis=2)
    lift_size = 0.5 * math.log(STATE * SPELL_LENGTH) + 0.43 * math.sqrt(SPELL_LENGTH / STATE)
    return (jitter + displacement + jnp.where(marked_indicator[:, :, None], lift_size, 0.0)).astype(jnp.bfloat16)


def shard_levels(own_key, extent, cuts, least, largest):
    loudness = 1.0
    for axis_at, parts in cuts:
        steps = jax.random.uniform(jax.random.fold_in(jax.random.fold_in(own_key, 6), axis_at), (parts,), jnp.float32, least / len(cuts), largest / len(cuts))
        loudness = loudness * jnp.repeat(jnp.exp(steps), extent[axis_at] // parts).reshape((-1,) + (1,) * (len(extent) - 1 - axis_at))
    return loudness


def noise(rng, dims, deviation, reach, cuts=(), kind=jnp.bfloat16):
    values = jax.random.normal(rng, dims, jnp.float32) * deviation
    if len(cuts) > 0:
        values = shard_levels(rng, dims, cuts, -0.22, 0.18) * values
    return jnp.clip(values, min=-reach, max=reach).astype(kind)


def setup_inputs(seed: int = 0, part: int = 0) -> dict:
    streams_of = jax.random.split(jax.random.key(seed), 12)
    own_keys = jax.random.split(jax.random.fold_in(streams_of[11], part), 12)
    return {
        "x_raw": noise(own_keys[0], (NBLOCKS, ROWS, INNER), 1.0, 6.0, ((0, 8), (1, 2))),
        "bc_raw": noise(own_keys[1], (NBLOCKS, ROWS, 2 * GROUPS * STATE), 1.0, 6.0, ((0, 8), (1, 2))),
        "dt_raw": draw_dt_raw(jax.random.fold_in(jax.random.fold_in(streams_of[11], part), 71), part),
        "conv_x_weight": noise(streams_of[3], (CONV, INNER), CONV ** -0.5, 3.0, ((1, 2),), jnp.float32),
        "conv_x_bias": noise(streams_of[4], (INNER,), 0.3, 2.5, ((0, 2),), jnp.float32),
        "conv_bc_weight": noise(streams_of[5], (CONV, 2 * GROUPS * STATE), CONV ** -0.5, 3.0, ((1, 2),), jnp.float32),
        "conv_bc_bias": noise(streams_of[6], (2 * GROUPS * STATE,), 0.3, 2.5, ((0, 2),), jnp.float32),
        "stride_offset_per_head": draw_stride_offset_per_head(jax.random.fold_in(streams_of[11], 71), part),
        "a_log": draw_a_log(jax.random.fold_in(streams_of[11], 71), part),
        "skip_d": jnp.clip(0.5 + 1.0 * jax.random.uniform(streams_of[9], (HEADS,), jnp.float32) ** shard_levels(streams_of[9], (HEADS,), ((0, 2),), -0.2, 0.2), 0.5, 1.5),
        "norm_gain": jnp.clip(1.0 + 0.18 * jax.random.normal(streams_of[10], (INNER,), jnp.float32), 0.1, 1.9),
    }


NORM_EPSILON = 1e-05

def rounded(values):
    return lax.optimization_barrier(values.astype(jnp.bfloat16)).astype(jnp.float32)

def conv_rows(raw_rows, rim_rows, weight, bias):
    conv_width = weight.shape[0]
    row_count = raw_rows.shape[0]
    joined = jnp.concatenate([rim_rows, raw_rows], axis=0).astype(jnp.float32)
    running = bias[None, :]
    for tap_index in range(conv_width):
        running = running + weight[tap_index][None, :] * joined[tap_index:tap_index + row_count]
    return jax.nn.silu(running).astype(jnp.bfloat16)

def reference(x_raw, bc_raw, dt_raw, conv_x_weight, conv_x_bias, conv_bc_weight, conv_bc_bias, stride_offset_per_head, a_log, skip_d, norm_gain):
    blocks = SPELL_LENGTH // SPAN
    per_group = HEADS // GROUPS
    x_all = x_raw.reshape(blocks, SPAN, INNER)
    bc_all = bc_raw.reshape(blocks, SPAN, 2 * GROUPS * STATE)
    dt_all = dt_raw.reshape(blocks, SPAN, HEADS)
    causal = lax.broadcasted_iota(jnp.int32, (SPAN, SPAN), 0) >= lax.broadcasted_iota(jnp.int32, (SPAN, SPAN), 1)
    decay_rate = -jnp.exp(a_log)

    def one_block(running, block_item):
        carried_state, x_tail, bc_tail = running
        x_rows, bc_rows, dt_rows = block_item
        x_conv = conv_rows(x_rows, x_tail, conv_x_weight, conv_x_bias)
        bc_conv = conv_rows(bc_rows, bc_tail, conv_bc_weight, conv_bc_bias)
        dt_step = jax.nn.softplus(dt_rows.astype(jnp.float32) + stride_offset_per_head[None, :])
        cum_decay = jnp.cumsum(decay_rate[None, :] * dt_step, axis=0)
        x_heads = lax.optimization_barrier(x_conv).astype(jnp.float32).reshape(SPAN, GROUPS, per_group, HEAD_DIM)
        bc_heads = lax.optimization_barrier(bc_conv).astype(jnp.float32).reshape(SPAN, GROUPS, 2, STATE)
        b_in = bc_heads[:, :, 0]
        c_out = bc_heads[:, :, 1]
        inner_prod = jnp.einsum('tgn,sgn->gts', c_out, b_in)
        cum_heads = cum_decay.T.reshape(GROUPS, per_group, SPAN)
        step_heads = dt_step.T.reshape(GROUPS, per_group, SPAN)
        gap_pairs = cum_heads[..., :, None] - cum_heads[..., None, :]
        weight = jnp.exp(jnp.where(causal, gap_pairs, -1e+30)) * step_heads[..., None, :]
        mixing = rounded(inner_prod[:, None] * weight)
        within_block_output = jnp.einsum('gjts,sgjp->tgjp', mixing, x_heads)
        block_end = cum_decay[-1]
        to_end = jnp.exp(block_end[None, :] - cum_decay) * dt_step
        scaled = rounded(to_end.reshape(SPAN, GROUPS, per_group, 1) * x_heads)
        block_state = jnp.einsum('sgjp,sgn->gjpn', scaled, b_in)
        carried_bf = rounded(carried_state)
        y_state = jnp.einsum('tgn,gjpn->tgjp', c_out, carried_bf) * jnp.exp(cum_decay).reshape(SPAN, GROUPS, per_group, 1)
        complete_output = within_block_output + y_state + skip_d.reshape(GROUPS, per_group, 1) * x_heads
        squares_mean = lax.optimization_barrier(jnp.mean(complete_output * complete_output, axis=(2, 3)))
        normed = complete_output * lax.rsqrt(squares_mean + NORM_EPSILON)[:, :, None, None] * norm_gain.reshape(GROUPS, per_group, HEAD_DIM)
        new_state = jnp.exp(block_end).reshape(GROUPS, per_group, 1, 1) * carried_state + block_state
        tails = (x_rows[SPAN - CONV + 1:], bc_rows[SPAN - CONV + 1:])
        return ((new_state, tails[0], tails[1]), normed.reshape(SPAN, INNER).astype(jnp.bfloat16))
    start = (jnp.zeros((GROUPS, per_group, HEAD_DIM, STATE), jnp.float32), jnp.zeros((CONV - 1, INNER), x_raw.dtype), jnp.zeros((CONV - 1, 2 * GROUPS * STATE), bc_raw.dtype))
    final_carry, outputs = lax.scan(one_block, start, (x_all, bc_all, dt_all))
    return outputs.reshape(NBLOCKS, ROWS, INNER)
```

```python
import functools
import jax
import jax.numpy as jnp
from jax import lax
from jax.experimental import pallas as pl
from jax.experimental.pallas import tpu as pltpu
from jax.sharding import PartitionSpec as P

STATE = 128
SPAN = 128
HEAD_DIM = 64
PER_GROUP = 16
WIDE = PER_GROUP * HEAD_DIM
PAIRS = PER_GROUP // 2
NORM_EPSILON = 1e-05
MESH = pl.DeviceIdType.MESH
F32 = jnp.float32
BF16 = jnp.bfloat16


def kernel(nseq, nhead, x_ref, bc_ref, dt_ref, wx_ref, bx_ref, wb_ref, bb_ref, par_ref, gain_ref, out_ref,
           xf, bcf, dtf, xc, bcc, ext, tail32, tail_out, tail_in, cum_sc, dt_sc, cumt_sc, dtt_sc, par_sc,
           end_out, end_in, st, sb, s0, ein, eout, cb, ysc, ecw,
           x_s, x_r, b_s, b_r, d_s, d_r, t_s, t_r, e_s, e_r, s_s, s_r, c_s, c_r, f_s, f_r):
    seq = lax.axis_index("seq")
    head = lax.axis_index("head")
    sub = lax.axis_index("sub")
    rows = x_ref.shape[1]
    groups = xf.shape[0]
    width = groups * WIDE
    bcw = groups * 2 * STATE
    heads = groups * PER_GROUP
    not_first = jnp.logical_or(seq > 0, sub > 0)
    not_last = jnp.logical_or(seq < nseq - 1, sub < 1)
    holds_tail = jnp.logical_and(not_last, head == nhead - 1)
    next_seq, prev_seq = seq + sub, seq + sub - 1
    other = 1 - sub
    lower, upper = sub == 0, sub == 1
    chain_in = jnp.logical_and(upper, seq > 0)
    chain_out = jnp.logical_and(upper, seq < nseq - 1)
    fwd_in = jnp.logical_and(lower, seq > 0)

    barrier = pltpu.get_barrier_semaphore()

    def tell(**where):
        pl.semaphore_signal(barrier, inc=1, device_id=where, device_id_type=MESH)

    partners = [lax.rem(head + d, nhead) for d in range(1, nhead)]
    for p in partners:
        tell(head=p)

    @pl.when(not_first)
    def _():
        tell(seq=prev_seq, sub=other, head=nhead - 1)

    @pl.when(upper)
    def _():
        tell(sub=0)

    @pl.when(fwd_in)
    def _():
        tell(sub=1)

    @pl.when(chain_in)
    def _():
        tell(seq=seq - 1)

    tail32[...] = jnp.zeros_like(tail32)
    for k in range(nhead):
        for j in range(groups):
            lo = k * width + j * WIDE
            tail32[3 * j:3 * j + 3, :] = x_ref[0, rows - 16:rows, lo:lo + WIDE].astype(F32)[13:16, :]
        lo = k * bcw
        tail32[12:15, 0:bcw] = bc_ref[0, rows - 16:rows, lo:lo + bcw].astype(F32)[13:16, :]
        tail_out[k] = tail32[...].astype(BF16)

    one = lambda cond: jnp.where(cond, 1, 0).astype(jnp.int32)
    peers = nhead - 1 + nhead * one(holds_tail) + one(lower) + one(chain_in) + one(chain_out)
    pl.semaphore_wait(barrier, peers)

    def remote(src, dst, send, recv, **where):
        return pltpu.make_async_remote_copy(
            src_ref=src, dst_ref=dst, send_sem=send, recv_sem=recv, device_id=where, device_id_type=MESH)

    mine = pl.ds(pl.multiple_of(head * rows, rows), rows)

    def x_copy(d, g):
        at = pl.ds(pl.multiple_of(partners[d] * width + g * WIDE, WIDE), WIDE)
        return remote(x_ref.at[0, :, at], xf.at[g, mine, :], x_s.at[d, g], x_r.at[d, g], head=partners[d])

    def bc_copy(d, g):
        at = pl.ds(pl.multiple_of(partners[d] * bcw + g * 2 * STATE, 2 * STATE), 2 * STATE)
        return remote(bc_ref.at[0, :, at], bcf.at[g, mine, :], b_s.at[d, g], b_r.at[d, g], head=partners[d])

    def dt_copy(d):
        return remote(dt_ref.at[0], dtf.at[mine, :], d_s.at[d], d_r.at[d], head=partners[d])

    def tail_copy(k):
        return remote(tail_out.at[k], tail_in, t_s.at[k], t_r, seq=next_seq, sub=other, head=k)

    def end_copy():
        return remote(end_out, end_in, e_s, e_r, sub=other)

    def s_copy(g):
        return remote(sb.at[g], s0.at[g], s_s.at[g], s_r.at[g], sub=other)

    def chain_copy(g):
        return remote(eout.at[g], ein.at[g], c_s.at[g], c_r.at[g], seq=seq + 1)

    def fwd_copy(g):
        return remote(ein.at[g], ein.at[g], f_s.at[g], f_r.at[g], sub=other)

    for d in range(nhead - 1):
        dt_copy(d).start()

    @pl.when(holds_tail)
    def _():
        for k in range(nhead):
            tail_copy(k).start()

    for g in range(groups):
        for d in range(nhead - 1):
            bc_copy(d, g).start()
            x_copy(d, g).start()

    for g in range(groups):
        at = pl.ds(pl.multiple_of(head * width + g * WIDE, WIDE), WIDE)
        xf[g, mine, :] = x_ref[0, :, at]
        at = pl.ds(pl.multiple_of(head * bcw + g * 2 * STATE, 2 * STATE), 2 * STATE)
        bcf[g, mine, :] = bc_ref[0, :, at]
    dtf[mine, :] = dt_ref[0]

    @pl.when(jnp.logical_not(not_first))
    def _():
        tail_in[...] = jnp.zeros_like(tail_in)

    @pl.when(seq == 0)
    def _():
        ein[...] = jnp.zeros_like(ein)

    for d in range(nhead - 1):
        dt_copy(d).wait_recv()
    dt_all = dtf[...].astype(F32)
    dt_own = dt_all
    for k in range(1, nhead):
        dt_own = jnp.where(head == k, pltpu.roll(dt_all, 128 - k * heads, 1), dt_own)
    par = par_ref[...]
    v = dt_own + par[0:1, :]
    u = jnp.exp(-jnp.abs(v))
    series = u * (1.0 - u * (0.5 - u * (1.0 / 3.0 - u * 0.25)))
    step = jnp.maximum(v, 0.0) + jnp.where(u < 0.03, series, jnp.log(1.0 + u))
    rate = -jnp.exp(par[1:2, :])
    row = lax.broadcasted_iota(jnp.int32, (SPAN, SPAN), 0)
    col = lax.broadcasted_iota(jnp.int32, (SPAN, SPAN), 1)
    causal = row >= col
    cum = jnp.dot(jnp.where(causal, 1.0, 0.0).astype(F32), rate * step,
                  preferred_element_type=F32, precision=lax.Precision.HIGHEST)
    cumt_sc[...] = jnp.transpose(cum)
    dtt_sc[...] = jnp.transpose(step)
    for g in range(groups):
        turn = (128 - g * PER_GROUP) % 128
        cum_g = pltpu.roll(cum, turn, 1) if turn else cum
        cum_sc[g] = cum_g
        dt_sc[g] = pltpu.roll(step, turn, 1) if turn else step
        par_sc[g] = pltpu.roll(par, turn, 1) if turn else par
        end_out[g] = jnp.broadcast_to(cum_g[SPAN - 1:SPAN, :], (8, 128))

    @pl.when(lower)
    def _():
        end_copy().start()

    @pl.when(upper)
    def _():
        end_copy().wait_recv()

    @pl.when(not_first)
    def _():
        tail_copy(0).wait_recv()

    tail32[...] = tail_in[...].astype(F32)
    left = col < HEAD_DIM

    def pair_wide(per_head, p):
        n = per_head.shape[0]
        a = jnp.broadcast_to(per_head[:, 2 * p:2 * p + 1], (n, 128))
        b = jnp.broadcast_to(per_head[:, 2 * p + 1:2 * p + 2], (n, 128))
        return jnp.where(left[0:n], a, b)

    def wide_row(per_head):
        return jnp.concatenate([pair_wide(per_head, p) for p in range(PAIRS)], axis=1)

    def conv(first, weights, bias, n):
        total = bias
        for k in range(4):
            total = total + weights[k:k + 1, :] * ext[5 + k:5 + k + SPAN, first:first + n]
        return (total * (1.0 / (1.0 + jnp.exp(-total)))).astype(BF16)

    for g in range(groups):
        for d in range(nhead - 1):
            bc_copy(d, g).wait_recv()
            x_copy(d, g).wait_recv()
        lo = g * WIDE
        blo = g * 2 * STATE
        ext[8:8 + SPAN, 0:WIDE] = xf[g].astype(F32)
        ext[8:8 + SPAN, WIDE:WIDE + 2 * STATE] = bcf[g].astype(F32)
        ext[5:8, 0:WIDE] = tail32[3 * g:3 * g + 3, :]
        ext[5:8, WIDE:WIDE + 2 * STATE] = tail32[12:15, blo:blo + 2 * STATE]
        bcc[g] = conv(WIDE, wb_ref[:, blo:blo + 2 * STATE], bb_ref[:, blo:blo + 2 * STATE], 2 * STATE)
        b_in = bcc[g, :, 0:STATE]
        for p in range(PAIRS):
            q = p * 128
            xcp = conv(q, wx_ref[:, lo + q:lo + q + 128], bx_ref[:, lo + q:lo + q + 128], 128)
            xc[g, :, q:q + 128] = xcp
            cum_p = pair_wide(cum_sc[g], p)
            ecw[g, :, q:q + 128] = jnp.exp(cum_p)
            to_end = jnp.exp(cum_p[SPAN - 1:SPAN, :] - cum_p) * pair_wide(dt_sc[g], p)
            cb[g, :, q:q + 128] = (to_end * xcp.astype(F32)).astype(BF16)
        state = lax.dot_general(b_in, cb[g], (((0,), (0,)), ((), ())), preferred_element_type=F32)

        @pl.when(lower)
        def _(state=state, g=g):
            sb[g] = state.astype(BF16)
            s_copy(g).start()

        @pl.when(upper)
        def _(state=state, g=g):
            st[g] = state

    def second(g, carry):
        @pl.when(upper)
        def _():
            @pl.when(chain_in)
            def _():
                chain_in_wait = remote(eout.at[g], ein.at[g], c_s.at[g], c_r.at[g], sub=other)
                chain_in_wait.wait_recv()
                fwd_copy(g).start()

            s_copy(g).wait_recv()
            d0 = jnp.exp(wide_row(end_in[g]))[0:1, :]
            d1 = jnp.exp(wide_row(end_out[g]))[0:1, :]
            carried = d0 * ein[g].astype(F32) + s0[g].astype(F32)
            cb[g] = carried.astype(BF16)

            @pl.when(chain_out)
            def _():
                eout[g] = (d1 * carried + st[g]).astype(BF16)
                chain_copy(g).start()

        inner = lax.dot_general(bcc[g, :, STATE:], bcc[g, :, 0:STATE], (((1,), (1,)), ((), ())),
                                preferred_element_type=F32)
        at = pl.ds(pl.multiple_of(g * PER_GROUP, PER_GROUP), PER_GROUP)
        cum_rows, dt_rows = cumt_sc[at, :], dtt_sc[at, :]
        cum_g = cum_sc[g]
        skip = par_sc[g]
        for p in range(PAIRS):
            mix = []
            for j in (2 * p, 2 * p + 1):
                gap = jnp.broadcast_to(cum_g[:, j:j + 1], (SPAN, SPAN)) - cum_rows[j:j + 1, :]
                w = jnp.exp(jnp.where(causal, gap, -1e30)) * dt_rows[j:j + 1, :]
                mix.append((inner * w).astype(BF16))
            xp = xc[g, :, p * 128:(p + 1) * 128]
            y = jnp.dot(jnp.concatenate(mix, axis=0), xp, preferred_element_type=F32)
            y = jnp.where(left, y[0:SPAN], y[SPAN:])
            ysc[g, :, p * 128:(p + 1) * 128] = y + pair_wide(skip, p)[2:3, :] * xp.astype(F32)
        return carry

    lax.fori_loop(0, groups, second, 0)

    def third(g, carry):
        @pl.when(lower)
        def _():
            @pl.when(fwd_in)
            def _():
                fwd_copy(g).wait_recv()

            cb[g] = ein[g]

        y = jnp.dot(bcc[g, :, STATE:], cb[g], preferred_element_type=F32)
        y = y * ecw[g] + ysc[g]
        mean = jnp.mean(y * y, axis=1, keepdims=True)
        at = pl.ds(pl.multiple_of(g * WIDE, WIDE), WIDE)
        out_ref[0, :, at] = (y * lax.rsqrt(mean + NORM_EPSILON) * gain_ref[:, at]).astype(BF16)
        return carry

    lax.fori_loop(0, groups, third, 0)

    for d in range(nhead - 1):
        dt_copy(d).wait_send()
        for g in range(groups):
            bc_copy(d, g).wait_send()
            x_copy(d, g).wait_send()

    @pl.when(holds_tail)
    def _():
        for k in range(nhead):
            tail_copy(k).wait_send()

    @pl.when(lower)
    def _():
        end_copy().wait_send()
        for g in range(groups):
            s_copy(g).wait_send()

    @pl.when(chain_in)
    def _():
        for g in range(groups):
            fwd_copy(g).wait_send()

    @pl.when(chain_out)
    def _():
        for g in range(groups):
            chain_copy(g).wait_send()


def on_device(nseq, nhead, x_raw, bc_raw, dt_raw, conv_x_weight, conv_x_bias, conv_bc_weight, conv_bc_bias,
              stride_offset_per_head, a_log, skip_d, norm_gain):
    width = conv_x_weight.shape[1]
    groups = width // WIDE
    heads = a_log.shape[0]
    par = jnp.pad(jnp.stack([stride_offset_per_head, a_log, skip_d]), ((0, 5), (0, 128 - heads)))
    V = pltpu.VMEM
    dma = lambda *s: pltpu.SemaphoreType.DMA(s)
    g3 = (groups, STATE, WIDE)
    return pl.pallas_call(
        functools.partial(kernel, nseq, nhead),
        out_shape=jax.ShapeDtypeStruct((1, SPAN, width), BF16),
        in_specs=[pl.BlockSpec(memory_space=pltpu.VMEM)] * 9,
        out_specs=pl.BlockSpec(memory_space=pltpu.VMEM),
        scratch_shapes=[
            V(g3, BF16), V((groups, SPAN, 2 * STATE), BF16), V((SPAN, 128), BF16),
            V(g3, BF16), V((groups, SPAN, 2 * STATE), BF16), V((SPAN + 8, WIDE + 2 * STATE), F32),
            V((16, WIDE), F32), V((nhead, 16, WIDE), BF16), V((16, WIDE), BF16),
            V((groups, SPAN, 128), F32), V((groups, SPAN, 128), F32), V((128, SPAN), F32), V((128, SPAN), F32),
            V((groups, 8, 128), F32), V((groups, 8, 128), F32), V((groups, 8, 128), F32),
            V(g3, F32), V(g3, BF16), V(g3, BF16), V(g3, BF16), V(g3, BF16), V(g3, BF16), V(g3, F32), V(g3, F32),
            dma(nhead - 1, groups), dma(nhead - 1, groups), dma(nhead - 1, groups), dma(nhead - 1, groups),
            dma(nhead - 1), dma(nhead - 1), dma(nhead), pltpu.SemaphoreType.DMA,
            pltpu.SemaphoreType.DMA, pltpu.SemaphoreType.DMA, dma(groups), dma(groups),
            dma(groups), dma(groups), dma(groups), dma(groups),
        ],
        compiler_params=pltpu.CompilerParams(
            collective_id=0, has_side_effects=True, vmem_limit_bytes=48 * 1024 * 1024),
    )(x_raw, bc_raw, dt_raw, conv_x_weight, conv_x_bias[None], conv_bc_weight, conv_bc_bias[None], par,
      norm_gain[None])


def solution(mesh):
    placed = (
        P(("groups", "seq", "sub"), "head", None),
        P(("groups", "seq", "sub"), "head", None),
        P(("groups", "seq", "sub"), "head", None),
        P(None, "head"),
        P("head"),
        P(None, "head"),
        P("head"),
        P("head"),
        P("head"),
        P("head"),
        P("head"),
    )
    return jax.shard_map(
        functools.partial(on_device, mesh.shape["seq"], mesh.shape["head"]),
        mesh=mesh,
        in_specs=placed,
        out_specs=P(("groups", "seq", "sub"), None, "head"),
        check_vma=False,
    )
```

```python
import functools
import jax
import jax.numpy as jnp
from jax import lax
from jax.experimental import pallas as pl
from jax.experimental.pallas import tpu as pltpu
from jax.sharding import PartitionSpec as P

STATE = 128
SPAN = 128
HEAD_DIM = 64
PER_GROUP = 16
WIDE = PER_GROUP * HEAD_DIM
PAIRS = PER_GROUP // 2
NORM_EPSILON = 1e-05
MESH = pl.DeviceIdType.MESH
F32 = jnp.float32
BF16 = jnp.bfloat16


def kernel(nseq, nhead, x_ref, bc_ref, dt_ref, wx_hbm, bx_hbm, wb_hbm, bb_hbm, par_hbm, gain_hbm, out_ref,
           wx_ref, bx_ref, wb_ref, bb_ref, par_ref, gain_ref, x_last, bc_last, par_l, x_l, b_l,
           xf, bcf, dtf, xc, bcc, ext, tail32, tail_out, tail_in, cum_sc, dt_sc, cumt_sc, dtt_sc, par_sc,
           end_out, end_in, st, sb, s0, ein, eout, cb, ysc, ecw,
           x_s, x_r, b_s, b_r, d_s, d_r, t_s, t_r, e_s, e_r, s_s, s_r, c_s, c_r, f_s, f_r):
    seq = lax.axis_index("seq")
    head = lax.axis_index("head")
    sub = lax.axis_index("sub")
    rows = x_ref.shape[1]
    groups = xf.shape[0]
    width = groups * WIDE
    bcw = groups * 2 * STATE
    heads = groups * PER_GROUP
    not_first = jnp.logical_or(seq > 0, sub > 0)
    not_last = jnp.logical_or(seq < nseq - 1, sub < 1)
    holds_tail = jnp.logical_and(not_last, head == nhead - 1)
    next_seq, prev_seq = seq + sub, seq + sub - 1
    other = 1 - sub
    lower, upper = sub == 0, sub == 1
    chain_in = jnp.logical_and(upper, seq > 0)
    chain_out = jnp.logical_and(upper, seq < nseq - 1)
    fwd_in = jnp.logical_and(lower, seq > 0)

    barrier = pltpu.get_barrier_semaphore()

    def tell(**where):
        pl.semaphore_signal(barrier, inc=1, device_id=where, device_id_type=MESH)

    partners = [lax.rem(head + d, nhead) for d in range(1, nhead)]
    for p in partners:
        tell(head=p)

    @pl.when(not_first)
    def _():
        tell(seq=prev_seq, sub=other, head=nhead - 1)

    @pl.when(upper)
    def _():
        tell(sub=0)

    @pl.when(fwd_in)
    def _():
        tell(sub=1)

    @pl.when(chain_in)
    def _():
        tell(seq=seq - 1)

    local = []
    for src, dst in ((x_ref.at[0, pl.ds(rows - 16, 16), :], x_last), (bc_ref.at[0, pl.ds(rows - 16, 16), :], bc_last),
                     (par_hbm, par_ref), (wx_hbm, wx_ref), (bx_hbm, bx_ref), (wb_hbm, wb_ref), (bb_hbm, bb_ref),
                     (gain_hbm, gain_ref)):
        local.append(pltpu.make_async_copy(src, dst, par_l.at[len(local)]))
    mine = pl.ds(pl.multiple_of(head * rows, rows), rows)
    local.append(pltpu.make_async_copy(dt_ref.at[0], dtf.at[mine, :], par_l.at[len(local)]))
    own = []
    for g in range(groups):
        at = pl.ds(pl.multiple_of(head * width + g * WIDE, WIDE), WIDE)
        bat = pl.ds(pl.multiple_of(head * bcw + g * 2 * STATE, 2 * STATE), 2 * STATE)
        own.append((pltpu.make_async_copy(x_ref.at[0, :, at], xf.at[g, mine, :], x_l.at[g]),
                    pltpu.make_async_copy(bc_ref.at[0, :, bat], bcf.at[g, mine, :], b_l.at[g])))
    for copy in local:
        copy.start()

    local[0].wait()
    local[1].wait()
    tail32[...] = jnp.zeros_like(tail32)
    for k in range(nhead):
        for j in range(groups):
            lo = k * width + j * WIDE
            tail32[3 * j:3 * j + 3, :] = x_last[:, lo:lo + WIDE].astype(F32)[13:16, :]
        lo = k * bcw
        tail32[12:15, 0:bcw] = bc_last[:, lo:lo + bcw].astype(F32)[13:16, :]
        tail_out[k] = tail32[...].astype(BF16)

    one = lambda cond: jnp.where(cond, 1, 0).astype(jnp.int32)
    peers = nhead - 1 + nhead * one(holds_tail) + one(lower) + one(chain_in) + one(chain_out)
    pl.semaphore_wait(barrier, peers)

    def remote(src, dst, send, recv, **where):
        return pltpu.make_async_remote_copy(
            src_ref=src, dst_ref=dst, send_sem=send, recv_sem=recv, device_id=where, device_id_type=MESH)

    def x_copy(d, g):
        at = pl.ds(pl.multiple_of(partners[d] * width + g * WIDE, WIDE), WIDE)
        return remote(x_ref.at[0, :, at], xf.at[g, mine, :], x_s.at[d, g], x_r.at[d, g], head=partners[d])

    def bc_copy(d, g):
        at = pl.ds(pl.multiple_of(partners[d] * bcw + g * 2 * STATE, 2 * STATE), 2 * STATE)
        return remote(bc_ref.at[0, :, at], bcf.at[g, mine, :], b_s.at[d, g], b_r.at[d, g], head=partners[d])

    def dt_copy(d):
        return remote(dt_ref.at[0], dtf.at[mine, :], d_s.at[d], d_r.at[d], head=partners[d])

    def tail_copy(k):
        return remote(tail_out.at[k], tail_in, t_s.at[k], t_r, seq=next_seq, sub=other, head=k)

    def end_copy():
        return remote(end_out, end_in, e_s, e_r, sub=other)

    def s_copy(g):
        return remote(sb.at[g], s0.at[g], s_s.at[g], s_r.at[g], sub=other)

    def chain_copy(g):
        return remote(eout.at[g], ein.at[g], c_s.at[g], c_r.at[g], seq=seq + 1)

    def fwd_copy(g):
        return remote(ein.at[g], ein.at[g], f_s.at[g], f_r.at[g], sub=other)

    for d in range(nhead - 1):
        dt_copy(d).start()

    @pl.when(holds_tail)
    def _():
        for k in range(nhead):
            tail_copy(k).start()

    for g in range(groups):
        for d in range(nhead - 1):
            bc_copy(d, g).start()
            x_copy(d, g).start()

    for x_own, bc_own in own:
        bc_own.start()
        x_own.start()

    @pl.when(jnp.logical_not(not_first))
    def _():
        tail_in[...] = jnp.zeros_like(tail_in)

    @pl.when(seq == 0)
    def _():
        ein[...] = jnp.zeros_like(ein)

    for d in range(nhead - 1):
        dt_copy(d).wait_recv()
    for copy in local[2:]:
        copy.wait()
    dt_all = dtf[...].astype(F32)
    dt_own = dt_all
    for k in range(1, nhead):
        dt_own = jnp.where(head == k, pltpu.roll(dt_all, 128 - k * heads, 1), dt_own)
    par = par_ref[...]
    v = dt_own + par[0:1, :]
    u = jnp.exp(-jnp.abs(v))
    series = u * (1.0 - u * (0.5 - u * (1.0 / 3.0 - u * 0.25)))
    step = jnp.maximum(v, 0.0) + jnp.where(u < 0.03, series, jnp.log(1.0 + u))
    rate = -jnp.exp(par[1:2, :])
    row = lax.broadcasted_iota(jnp.int32, (SPAN, SPAN), 0)
    col = lax.broadcasted_iota(jnp.int32, (SPAN, SPAN), 1)
    causal = row >= col
    cum = jnp.dot(jnp.where(causal, 1.0, 0.0).astype(F32), rate * step,
                  preferred_element_type=F32, precision=lax.Precision.HIGHEST)
    cumt_sc[...] = jnp.transpose(cum)
    dtt_sc[...] = jnp.transpose(step)
    for g in range(groups):
        turn = (128 - g * PER_GROUP) % 128
        cum_g = pltpu.roll(cum, turn, 1) if turn else cum
        cum_sc[g] = cum_g
        dt_sc[g] = pltpu.roll(step, turn, 1) if turn else step
        par_sc[g] = pltpu.roll(par, turn, 1) if turn else par
        end_out[g] = jnp.broadcast_to(cum_g[SPAN - 1:SPAN, :], (8, 128))

    @pl.when(lower)
    def _():
        end_copy().start()

    @pl.when(upper)
    def _():
        end_copy().wait_recv()

    @pl.when(not_first)
    def _():
        tail_copy(0).wait_recv()

    tail32[...] = tail_in[...].astype(F32)
    left = col < HEAD_DIM

    def pair_wide(per_head, p):
        n = per_head.shape[0]
        a = jnp.broadcast_to(per_head[:, 2 * p:2 * p + 1], (n, 128))
        b = jnp.broadcast_to(per_head[:, 2 * p + 1:2 * p + 2], (n, 128))
        return jnp.where(left[0:n], a, b)

    def wide_row(per_head):
        return jnp.concatenate([pair_wide(per_head, p) for p in range(PAIRS)], axis=1)

    def conv(first, weights, bias, n):
        total = bias
        for k in range(4):
            total = total + weights[k:k + 1, :] * ext[5 + k:5 + k + SPAN, first:first + n]
        return (total * (1.0 / (1.0 + jnp.exp(-total)))).astype(BF16)

    lag = jnp.minimum(1 + 2 * seq, 2 * groups)

    def chain(slot):
        g = slot - lag

        @pl.when(jnp.logical_and(upper, jnp.logical_and(g >= 0, g < groups)))
        def _():
            @pl.when(chain_in)
            def _():
                remote(eout.at[g], ein.at[g], c_s.at[g], c_r.at[g], sub=other).wait_recv()
                fwd_copy(g).start()

            s_copy(g).wait_recv()
            d0 = jnp.exp(wide_row(end_in[g]))[0:1, :]
            d1 = jnp.exp(wide_row(end_out[g]))[0:1, :]
            carried = d0 * ein[g].astype(F32) + s0[g].astype(F32)
            cb[g] = carried.astype(BF16)

            @pl.when(chain_out)
            def _():
                eout[g] = (d1 * carried + st[g]).astype(BF16)
                chain_copy(g).start()

    for g in range(groups):
        own[g][0].wait()
        own[g][1].wait()
        for d in range(nhead - 1):
            bc_copy(d, g).wait_recv()
            x_copy(d, g).wait_recv()
        lo = g * WIDE
        blo = g * 2 * STATE
        ext[8:8 + SPAN, 0:WIDE] = xf[g].astype(F32)
        ext[8:8 + SPAN, WIDE:WIDE + 2 * STATE] = bcf[g].astype(F32)
        ext[5:8, 0:WIDE] = tail32[3 * g:3 * g + 3, :]
        ext[5:8, WIDE:WIDE + 2 * STATE] = tail32[12:15, blo:blo + 2 * STATE]
        bcc[g] = conv(WIDE, wb_ref[:, blo:blo + 2 * STATE], bb_ref[:, blo:blo + 2 * STATE], 2 * STATE)
        b_in = bcc[g, :, 0:STATE]
        for p in range(PAIRS):
            q = p * 128
            xcp = conv(q, wx_ref[:, lo + q:lo + q + 128], bx_ref[:, lo + q:lo + q + 128], 128)
            xc[g, :, q:q + 128] = xcp
            cum_p = pair_wide(cum_sc[g], p)
            ecw[g, :, q:q + 128] = jnp.exp(cum_p)
            to_end = jnp.exp(cum_p[SPAN - 1:SPAN, :] - cum_p) * pair_wide(dt_sc[g], p)
            cb[g, :, q:q + 128] = (to_end * xcp.astype(F32)).astype(BF16)
        state = lax.dot_general(b_in, cb[g], (((0,), (0,)), ((), ())), preferred_element_type=F32)

        @pl.when(lower)
        def _(state=state, g=g):
            sb[g] = state.astype(BF16)
            s_copy(g).start()

        @pl.when(upper)
        def _(state=state, g=g):
            st[g] = state

        chain(g)

    def second(g, carry):
        inner = lax.dot_general(bcc[g, :, STATE:], bcc[g, :, 0:STATE], (((1,), (1,)), ((), ())),
                                preferred_element_type=F32)
        at = pl.ds(pl.multiple_of(g * PER_GROUP, PER_GROUP), PER_GROUP)
        cum_rows, dt_rows = cumt_sc[at, :], dtt_sc[at, :]
        cum_g = cum_sc[g]
        skip = par_sc[g]
        for p in range(PAIRS):
            mix = []
            for j in (2 * p, 2 * p + 1):
                gap = jnp.broadcast_to(cum_g[:, j:j + 1], (SPAN, SPAN)) - cum_rows[j:j + 1, :]
                w = jnp.exp(jnp.where(causal, gap, -1e30)) * dt_rows[j:j + 1, :]
                mix.append((inner * w).astype(BF16))
            xp = xc[g, :, p * 128:(p + 1) * 128]
            y = jnp.dot(jnp.concatenate(mix, axis=0), xp, preferred_element_type=F32)
            y = jnp.where(left, y[0:SPAN], y[SPAN:])
            ysc[g, :, p * 128:(p + 1) * 128] = y + pair_wide(skip, p)[2:3, :] * xp.astype(F32)
        chain(groups + g)
        return carry

    lax.fori_loop(0, groups, second, 0)

    def third(g, carry):
        chain(2 * groups + g)

        @pl.when(lower)
        def _():
            @pl.when(fwd_in)
            def _():
                fwd_copy(g).wait_recv()

            cb[g] = ein[g]

        y = jnp.dot(bcc[g, :, STATE:], cb[g], preferred_element_type=F32)
        y = y * ecw[g] + ysc[g]
        mean = jnp.mean(y * y, axis=1, keepdims=True)
        at = pl.ds(pl.multiple_of(g * WIDE, WIDE), WIDE)
        out_ref[0, :, at] = (y * lax.rsqrt(mean + NORM_EPSILON) * gain_ref[:, at]).astype(BF16)
        return carry

    lax.fori_loop(0, groups, third, 0)

    for d in range(nhead - 1):
        dt_copy(d).wait_send()
        for g in range(groups):
            bc_copy(d, g).wait_send()
            x_copy(d, g).wait_send()

    @pl.when(holds_tail)
    def _():
        for k in range(nhead):
            tail_copy(k).wait_send()

    @pl.when(lower)
    def _():
        end_copy().wait_send()
        for g in range(groups):
            s_copy(g).wait_send()

    @pl.when(chain_in)
    def _():
        for g in range(groups):
            fwd_copy(g).wait_send()

    @pl.when(chain_out)
    def _():
        for g in range(groups):
            chain_copy(g).wait_send()


def on_device(nseq, nhead, x_raw, bc_raw, dt_raw, conv_x_weight, conv_x_bias, conv_bc_weight, conv_bc_bias,
              stride_offset_per_head, a_log, skip_d, norm_gain):
    width = conv_x_weight.shape[1]
    groups = width // WIDE
    heads = a_log.shape[0]
    par = jnp.pad(jnp.stack([stride_offset_per_head, a_log, skip_d]), ((0, 5), (0, 128 - heads)))
    V = pltpu.VMEM
    dma = lambda *s: pltpu.SemaphoreType.DMA(s)
    g3 = (groups, STATE, WIDE)
    return pl.pallas_call(
        functools.partial(kernel, nseq, nhead),
        out_shape=jax.ShapeDtypeStruct((1, SPAN, width), BF16),
        in_specs=[pl.BlockSpec(memory_space=pltpu.HBM)] * 9,
        out_specs=pl.BlockSpec(memory_space=pltpu.VMEM),
        scratch_shapes=[
            V(conv_x_weight.shape, F32), V((1, width), F32), V(conv_bc_weight.shape, F32),
            V((1, conv_bc_weight.shape[1]), F32), V((8, 128), F32), V((1, width), F32),
            V((16, x_raw.shape[2]), BF16), V((16, bc_raw.shape[2]), BF16), dma(9), dma(groups), dma(groups),
            V(g3, BF16), V((groups, SPAN, 2 * STATE), BF16), V((SPAN, 128), BF16),
            V(g3, BF16), V((groups, SPAN, 2 * STATE), BF16), V((SPAN + 8, WIDE + 2 * STATE), F32),
            V((16, WIDE), F32), V((nhead, 16, WIDE), BF16), V((16, WIDE), BF16),
            V((groups, SPAN, 128), F32), V((groups, SPAN, 128), F32), V((128, SPAN), F32), V((128, SPAN), F32),
            V((groups, 8, 128), F32), V((groups, 8, 128), F32), V((groups, 8, 128), F32),
            V(g3, F32), V(g3, BF16), V(g3, BF16), V(g3, BF16), V(g3, BF16), V(g3, BF16), V(g3, F32), V(g3, F32),
            dma(nhead - 1, groups), dma(nhead - 1, groups), dma(nhead - 1, groups), dma(nhead - 1, groups),
            dma(nhead - 1), dma(nhead - 1), dma(nhead), pltpu.SemaphoreType.DMA,
            pltpu.SemaphoreType.DMA, pltpu.SemaphoreType.DMA, dma(groups), dma(groups),
            dma(groups), dma(groups), dma(groups), dma(groups),
        ],
        compiler_params=pltpu.CompilerParams(
            collective_id=0, has_side_effects=True, vmem_limit_bytes=64 * 1024 * 1024 - 131072),
    )(x_raw, bc_raw, dt_raw, conv_x_weight, conv_x_bias[None], conv_bc_weight, conv_bc_bias[None], par,
      norm_gain[None])


def solution(mesh):
    placed = (
        P(("groups", "seq", "sub"), "head", None),
        P(("groups", "seq", "sub"), "head", None),
        P(("groups", "seq", "sub"), "head", None),
        P(None, "head"),
        P("head"),
        P(None, "head"),
        P("head"),
        P("head"),
        P("head"),
        P("head"),
        P("head"),
    )
    return jax.shard_map(
        functools.partial(on_device, mesh.shape["seq"], mesh.shape["head"]),
        mesh=mesh,
        in_specs=placed,
        out_specs=P(("groups", "seq", "sub"), None, "head"),
        check_vma=False,
    )
```

```python
import functools
import jax
import jax.numpy as jnp
from jax import lax
from jax.experimental import pallas as pl
from jax.experimental.pallas import tpu as pltpu
from jax.sharding import PartitionSpec as P

STATE = 128
SPAN = 128
HEAD_DIM = 64
PER_GROUP = 16
WIDE = PER_GROUP * HEAD_DIM
PAIRS = PER_GROUP // 2
NORM_EPSILON = 1e-05
PARTS = 4
PART = STATE // PARTS
MESH = pl.DeviceIdType.MESH
F32 = jnp.float32
BF16 = jnp.bfloat16


def kernel(nseq, nhead, x_ref, bc_ref, dt_ref, wx_hbm, bx_hbm, wb_hbm, bb_hbm, par_hbm, gain_hbm, out_ref,
           wx_ref, bx_ref, wb_ref, bb_ref, par_ref, gain_ref, x_last, bc_last, par_l, x_l, b_l,
           xf, bcf, dtf, xc, bcc, ext, tail32, tail_out, tail_in, cum_sc, dt_sc, cumt_sc, dtt_sc, par_sc,
           end_out, end_in, st, sb, s0, ein, eout, cb, ysc, ecw,
           x_s, x_r, b_s, b_r, d_s, d_r, t_s, t_r, e_s, e_r, s_s, s_r, c_s, c_r, f_s, f_r):
    seq = lax.axis_index("seq")
    head = lax.axis_index("head")
    sub = lax.axis_index("sub")
    rows = x_ref.shape[1]
    groups = xf.shape[0]
    width = groups * WIDE
    bcw = groups * 2 * STATE
    heads = groups * PER_GROUP
    not_first = jnp.logical_or(seq > 0, sub > 0)
    not_last = jnp.logical_or(seq < nseq - 1, sub < 1)
    holds_tail = jnp.logical_and(not_last, head == nhead - 1)
    next_seq, prev_seq = seq + sub, seq + sub - 1
    other = 1 - sub
    lower, upper = sub == 0, sub == 1
    chain_in = jnp.logical_and(upper, seq > 0)
    chain_out = jnp.logical_and(upper, seq < nseq - 1)
    fwd_in = jnp.logical_and(lower, seq > 0)

    barrier = pltpu.get_barrier_semaphore()

    def tell(**where):
        pl.semaphore_signal(barrier, inc=1, device_id=where, device_id_type=MESH)

    partners = [lax.rem(head + d, nhead) for d in range(1, nhead)]
    for p in partners:
        tell(head=p)

    @pl.when(not_first)
    def _():
        tell(seq=prev_seq, sub=other, head=nhead - 1)

    @pl.when(upper)
    def _():
        tell(sub=0)

    @pl.when(fwd_in)
    def _():
        tell(sub=1)

    @pl.when(chain_in)
    def _():
        tell(seq=seq - 1)

    local = []
    for src, dst in ((x_ref.at[0, pl.ds(rows - 16, 16), :], x_last), (bc_ref.at[0, pl.ds(rows - 16, 16), :], bc_last),
                     (par_hbm, par_ref), (wx_hbm, wx_ref), (bx_hbm, bx_ref), (wb_hbm, wb_ref), (bb_hbm, bb_ref),
                     (gain_hbm, gain_ref)):
        local.append(pltpu.make_async_copy(src, dst, par_l.at[len(local)]))
    mine = pl.ds(pl.multiple_of(head * rows, rows), rows)
    local.append(pltpu.make_async_copy(dt_ref.at[0], dtf.at[mine, :], par_l.at[len(local)]))
    own = []
    for g in range(groups):
        at = pl.ds(pl.multiple_of(head * width + g * WIDE, WIDE), WIDE)
        bat = pl.ds(pl.multiple_of(head * bcw + g * 2 * STATE, 2 * STATE), 2 * STATE)
        own.append((pltpu.make_async_copy(x_ref.at[0, :, at], xf.at[g, mine, :], x_l.at[g]),
                    pltpu.make_async_copy(bc_ref.at[0, :, bat], bcf.at[g, mine, :], b_l.at[g])))
    for copy in local:
        copy.start()

    one = lambda cond: jnp.where(cond, 1, 0).astype(jnp.int32)
    peers = nhead - 1 + nhead * one(holds_tail) + one(lower) + one(chain_in) + one(chain_out)
    pl.semaphore_wait(barrier, peers)

    def remote(src, dst, send, recv, **where):
        return pltpu.make_async_remote_copy(
            src_ref=src, dst_ref=dst, send_sem=send, recv_sem=recv, device_id=where, device_id_type=MESH)

    def x_copy(d, g):
        at = pl.ds(pl.multiple_of(partners[d] * width + g * WIDE, WIDE), WIDE)
        return remote(x_ref.at[0, :, at], xf.at[g, mine, :], x_s.at[d, g], x_r.at[d, g], head=partners[d])

    def bc_copy(d, g):
        at = pl.ds(pl.multiple_of(partners[d] * bcw + g * 2 * STATE, 2 * STATE), 2 * STATE)
        return remote(bc_ref.at[0, :, at], bcf.at[g, mine, :], b_s.at[d, g], b_r.at[d, g], head=partners[d])

    def dt_copy(d):
        return remote(dt_ref.at[0], dtf.at[mine, :], d_s.at[d], d_r.at[d], head=partners[d])

    def tail_copy(k):
        return remote(tail_out.at[k], tail_in, t_s.at[k], t_r, seq=next_seq, sub=other, head=k)

    def end_copy():
        return remote(end_out, end_in, e_s, e_r, sub=other)

    def s_copy(g):
        return remote(sb.at[g], s0.at[g], s_s.at[g], s_r.at[g], sub=other)

    def chain_copy(g, i):
        at = pl.ds(i * PART, PART)
        return remote(eout.at[g, at], ein.at[g, at], c_s.at[g, i], c_r.at[g, i], seq=seq + 1)

    def fwd_copy(g, i):
        at = pl.ds(i * PART, PART)
        return remote(ein.at[g, at], ein.at[g, at], f_s.at[g, i], f_r.at[g, i], sub=other)

    for d in range(nhead - 1):
        dt_copy(d).start()
        bc_copy(d, 0).start()
        x_copy(d, 0).start()

    local[0].wait()
    local[1].wait()
    tail32[...] = jnp.zeros_like(tail32)
    for k in range(nhead):
        for j in range(groups):
            lo = k * width + j * WIDE
            tail32[3 * j:3 * j + 3, :] = x_last[:, lo:lo + WIDE].astype(F32)[13:16, :]
        lo = k * bcw
        tail32[12:15, 0:bcw] = bc_last[:, lo:lo + bcw].astype(F32)[13:16, :]
        tail_out[k] = tail32[...].astype(BF16)

    @pl.when(holds_tail)
    def _():
        for k in range(nhead):
            tail_copy(k).start()

    for g in range(1, groups):
        for d in range(nhead - 1):
            bc_copy(d, g).start()
            x_copy(d, g).start()

    for x_own, bc_own in own:
        bc_own.start()
        x_own.start()

    @pl.when(jnp.logical_not(not_first))
    def _():
        tail_in[...] = jnp.zeros_like(tail_in)

    @pl.when(seq == 0)
    def _():
        ein[...] = jnp.zeros_like(ein)

    for d in range(nhead - 1):
        dt_copy(d).wait_recv()
    for copy in local[2:]:
        copy.wait()
    dt_all = dtf[...].astype(F32)
    dt_own = dt_all
    for k in range(1, nhead):
        dt_own = jnp.where(head == k, pltpu.roll(dt_all, 128 - k * heads, 1), dt_own)
    par = par_ref[...]
    v = dt_own + par[0:1, :]
    u = jnp.exp(-jnp.abs(v))
    series = u * (1.0 - u * (0.5 - u * (1.0 / 3.0 - u * 0.25)))
    step = jnp.maximum(v, 0.0) + jnp.where(u < 0.03, series, jnp.log(1.0 + u))
    rate = -jnp.exp(par[1:2, :])
    row = lax.broadcasted_iota(jnp.int32, (SPAN, SPAN), 0)
    col = lax.broadcasted_iota(jnp.int32, (SPAN, SPAN), 1)
    causal = row >= col
    cum = jnp.dot(jnp.where(causal, 1.0, 0.0).astype(F32), rate * step,
                  preferred_element_type=F32, precision=lax.Precision.HIGHEST)
    cumt_sc[...] = jnp.transpose(cum)
    dtt_sc[...] = jnp.transpose(step)
    for g in range(groups):
        turn = (128 - g * PER_GROUP) % 128
        cum_g = pltpu.roll(cum, turn, 1) if turn else cum
        cum_sc[g] = cum_g
        dt_sc[g] = pltpu.roll(step, turn, 1) if turn else step
        par_sc[g] = pltpu.roll(par, turn, 1) if turn else par
        end_out[g] = jnp.broadcast_to(cum_g[SPAN - 1:SPAN, :], (8, 128))

    @pl.when(lower)
    def _():
        end_copy().start()

    @pl.when(upper)
    def _():
        end_copy().wait_recv()

    @pl.when(not_first)
    def _():
        tail_copy(0).wait_recv()

    tail32[...] = tail_in[...].astype(F32)
    left = col < HEAD_DIM

    def pair_wide(per_head, p):
        n = per_head.shape[0]
        a = jnp.broadcast_to(per_head[:, 2 * p:2 * p + 1], (n, 128))
        b = jnp.broadcast_to(per_head[:, 2 * p + 1:2 * p + 2], (n, 128))
        return jnp.where(left[0:n], a, b)

    def wide_row(per_head):
        return jnp.concatenate([pair_wide(per_head, p) for p in range(PAIRS)], axis=1)

    def conv(first, weights, bias, n):
        total = bias
        for k in range(4):
            total = total + weights[k:k + 1, :] * ext[5 + k:5 + k + SPAN, first:first + n]
        return (total * (1.0 / (1.0 + jnp.exp(-total)))).astype(BF16)

    lag = jnp.minimum(1 + 2 * seq, 2 * groups)

    def chain(slot):
        g = slot - lag

        @pl.when(jnp.logical_and(upper, jnp.logical_and(g >= 0, g < groups)))
        def _():
            s_copy(g).wait_recv()
            d0 = jnp.exp(wide_row(end_in[g]))[0:1, :]
            d1 = jnp.exp(wide_row(end_out[g]))[0:1, :]
            for i in range(PARTS):
                at = slice(i * PART, (i + 1) * PART)

                @pl.when(chain_in)
                def _(i=i):
                    chain_copy(g, i).wait_recv()
                    fwd_copy(g, i).start()

                carried = d0 * ein[g, at, :].astype(F32) + s0[g, at, :].astype(F32)
                cb[g, at, :] = carried.astype(BF16)

                @pl.when(chain_out)
                def _(i=i, at=at, carried=carried):
                    eout[g, at, :] = (d1 * carried + st[g, at, :]).astype(BF16)
                    chain_copy(g, i).start()

    for g in range(groups):
        own[g][0].wait()
        own[g][1].wait()
        for d in range(nhead - 1):
            bc_copy(d, g).wait_recv()
            x_copy(d, g).wait_recv()
        lo = g * WIDE
        blo = g * 2 * STATE
        ext[8:8 + SPAN, 0:WIDE] = xf[g].astype(F32)
        ext[8:8 + SPAN, WIDE:WIDE + 2 * STATE] = bcf[g].astype(F32)
        ext[5:8, 0:WIDE] = tail32[3 * g:3 * g + 3, :]
        ext[5:8, WIDE:WIDE + 2 * STATE] = tail32[12:15, blo:blo + 2 * STATE]
        bcc[g] = conv(WIDE, wb_ref[:, blo:blo + 2 * STATE], bb_ref[:, blo:blo + 2 * STATE], 2 * STATE)
        b_in = bcc[g, :, 0:STATE]
        for p in range(PAIRS):
            q = p * 128
            xcp = conv(q, wx_ref[:, lo + q:lo + q + 128], bx_ref[:, lo + q:lo + q + 128], 128)
            xc[g, :, q:q + 128] = xcp
            cum_p = pair_wide(cum_sc[g], p)
            ecw[g, :, q:q + 128] = jnp.exp(cum_p)
            to_end = jnp.exp(cum_p[SPAN - 1:SPAN, :] - cum_p) * pair_wide(dt_sc[g], p)
            cb[g, :, q:q + 128] = (to_end * xcp.astype(F32)).astype(BF16)
        state = lax.dot_general(b_in, cb[g], (((0,), (0,)), ((), ())), preferred_element_type=F32)

        @pl.when(lower)
        def _(state=state, g=g):
            sb[g] = state.astype(BF16)
            s_copy(g).start()

        @pl.when(upper)
        def _(state=state, g=g):
            st[g] = state

        chain(g)

    def second(g, carry):
        inner = lax.dot_general(bcc[g, :, STATE:], bcc[g, :, 0:STATE], (((1,), (1,)), ((), ())),
                                preferred_element_type=F32)
        at = pl.ds(pl.multiple_of(g * PER_GROUP, PER_GROUP), PER_GROUP)
        cum_rows, dt_rows = cumt_sc[at, :], dtt_sc[at, :]
        cum_g = cum_sc[g]
        skip = par_sc[g]
        for p in range(PAIRS):
            mix = []
            for j in (2 * p, 2 * p + 1):
                gap = jnp.broadcast_to(cum_g[:, j:j + 1], (SPAN, SPAN)) - cum_rows[j:j + 1, :]
                w = jnp.exp(jnp.where(causal, gap, -1e30)) * dt_rows[j:j + 1, :]
                mix.append((inner * w).astype(BF16))
            xp = xc[g, :, p * 128:(p + 1) * 128]
            y = jnp.dot(jnp.concatenate(mix, axis=0), xp, preferred_element_type=F32)
            y = jnp.where(left, y[0:SPAN], y[SPAN:])
            ysc[g, :, p * 128:(p + 1) * 128] = y + pair_wide(skip, p)[2:3, :] * xp.astype(F32)
        chain(groups + g)
        return carry

    lax.fori_loop(0, groups, second, 0)

    def third(g, carry):
        chain(2 * groups + g)

        @pl.when(lower)
        def _():
            @pl.when(fwd_in)
            def _():
                for i in range(PARTS):
                    fwd_copy(g, i).wait_recv()

            cb[g] = ein[g]

        y = jnp.dot(bcc[g, :, STATE:], cb[g], preferred_element_type=F32)
        y = y * ecw[g] + ysc[g]
        mean = jnp.mean(y * y, axis=1, keepdims=True)
        at = pl.ds(pl.multiple_of(g * WIDE, WIDE), WIDE)
        out_ref[0, :, at] = (y * lax.rsqrt(mean + NORM_EPSILON) * gain_ref[:, at]).astype(BF16)
        return carry

    lax.fori_loop(0, groups, third, 0)

    for d in range(nhead - 1):
        dt_copy(d).wait_send()
        for g in range(groups):
            bc_copy(d, g).wait_send()
            x_copy(d, g).wait_send()

    @pl.when(holds_tail)
    def _():
        for k in range(nhead):
            tail_copy(k).wait_send()

    @pl.when(lower)
    def _():
        end_copy().wait_send()
        for g in range(groups):
            s_copy(g).wait_send()

    @pl.when(chain_in)
    def _():
        for g in range(groups):
            for i in range(PARTS):
                fwd_copy(g, i).wait_send()

    @pl.when(chain_out)
    def _():
        for g in range(groups):
            for i in range(PARTS):
                chain_copy(g, i).wait_send()


def on_device(nseq, nhead, x_raw, bc_raw, dt_raw, conv_x_weight, conv_x_bias, conv_bc_weight, conv_bc_bias,
              stride_offset_per_head, a_log, skip_d, norm_gain):
    width = conv_x_weight.shape[1]
    groups = width // WIDE
    heads = a_log.shape[0]
    par = jnp.pad(jnp.stack([stride_offset_per_head, a_log, skip_d]), ((0, 5), (0, 128 - heads)))
    V = pltpu.VMEM
    dma = lambda *s: pltpu.SemaphoreType.DMA(s)
    g3 = (groups, STATE, WIDE)
    return pl.pallas_call(
        functools.partial(kernel, nseq, nhead),
        out_shape=jax.ShapeDtypeStruct((1, SPAN, width), BF16),
        in_specs=[pl.BlockSpec(memory_space=pltpu.HBM)] * 9,
        out_specs=pl.BlockSpec(memory_space=pltpu.VMEM),
        scratch_shapes=[
            V(conv_x_weight.shape, F32), V((1, width), F32), V(conv_bc_weight.shape, F32),
            V((1, conv_bc_weight.shape[1]), F32), V((8, 128), F32), V((1, width), F32),
            V((16, x_raw.shape[2]), BF16), V((16, bc_raw.shape[2]), BF16), dma(9), dma(groups), dma(groups),
            V(g3, BF16), V((groups, SPAN, 2 * STATE), BF16), V((SPAN, 128), BF16),
            V(g3, BF16), V((groups, SPAN, 2 * STATE), BF16), V((SPAN + 8, WIDE + 2 * STATE), F32),
            V((16, WIDE), F32), V((nhead, 16, WIDE), BF16), V((16, WIDE), BF16),
            V((groups, SPAN, 128), F32), V((groups, SPAN, 128), F32), V((128, SPAN), F32), V((128, SPAN), F32),
            V((groups, 8, 128), F32), V((groups, 8, 128), F32), V((groups, 8, 128), F32),
            V(g3, F32), V(g3, BF16), V(g3, BF16), V(g3, BF16), V(g3, BF16), V(g3, BF16), V(g3, F32), V(g3, F32),
            dma(nhead - 1, groups), dma(nhead - 1, groups), dma(nhead - 1, groups), dma(nhead - 1, groups),
            dma(nhead - 1), dma(nhead - 1), dma(nhead), pltpu.SemaphoreType.DMA,
            pltpu.SemaphoreType.DMA, pltpu.SemaphoreType.DMA, dma(groups), dma(groups),
            dma(groups, PARTS), dma(groups, PARTS), dma(groups, PARTS), dma(groups, PARTS),
        ],
        compiler_params=pltpu.CompilerParams(
            collective_id=0, has_side_effects=True, vmem_limit_bytes=64 * 1024 * 1024 - 131072),
    )(x_raw, bc_raw, dt_raw, conv_x_weight, conv_x_bias[None], conv_bc_weight, conv_bc_bias[None], par,
      norm_gain[None])


def solution(mesh):
    placed = (
        P(("groups", "seq", "sub"), "head", None),
        P(("groups", "seq", "sub"), "head", None),
        P(("groups", "seq", "sub"), "head", None),
        P(None, "head"),
        P("head"),
        P(None, "head"),
        P("head"),
        P("head"),
        P("head"),
        P("head"),
        P("head"),
    )
    return jax.shard_map(
        functools.partial(on_device, mesh.shape["seq"], mesh.shape["head"]),
        mesh=mesh,
        in_specs=placed,
        out_specs=P(("groups", "seq", "sub"), None, "head"),
        check_vma=False,
    )
```

```python
import functools
import jax
import jax.numpy as jnp
from jax import lax
from jax.experimental import pallas as pl
from jax.experimental.pallas import tpu as pltpu
from jax.sharding import PartitionSpec as P

STATE = 128
SPAN = 128
HEAD_DIM = 64
PER_GROUP = 16
WIDE = PER_GROUP * HEAD_DIM
PAIRS = PER_GROUP // 2
NORM_EPSILON = 1e-05
PARTS = 4
PART = STATE // PARTS
MESH = pl.DeviceIdType.MESH
F32 = jnp.float32
BF16 = jnp.bfloat16


def kernel(nseq, nhead, x_ref, bc_ref, dt_ref, wx_hbm, bx_hbm, wb_hbm, bb_hbm, par_hbm, gain_hbm, out_ref,
           wx_ref, bx_ref, wb_ref, bb_ref, par_ref, gain_ref, x_last, bc_last, par_l, x_l, b_l,
           xf, bcf, dtf, xc, bcc, ext, tail32, tail_out, tail_in, cum_sc, dt_sc, cumt_sc, dtt_sc, par_sc,
           end_out, end_in, st, sb, s0, ein, eout, cb, ysc, ecw,
           x_s, x_r, b_s, b_r, d_s, d_r, t_s, t_r, e_s, e_r, s_s, s_r, c_s, c_r, f_s, f_r):
    seq = lax.axis_index("seq")
    head = lax.axis_index("head")
    sub = lax.axis_index("sub")
    rows = x_ref.shape[1]
    groups = xf.shape[0]
    width = groups * WIDE
    bcw = groups * 2 * STATE
    heads = groups * PER_GROUP
    not_first = jnp.logical_or(seq > 0, sub > 0)
    not_last = jnp.logical_or(seq < nseq - 1, sub < 1)
    holds_tail = jnp.logical_and(not_last, head == nhead - 1)
    next_seq, prev_seq = seq + sub, seq + sub - 1
    other = 1 - sub
    lower, upper = sub == 0, sub == 1
    chain_in = jnp.logical_and(upper, seq > 0)
    chain_out = jnp.logical_and(upper, seq < nseq - 1)
    fwd_in = jnp.logical_and(lower, seq > 0)

    barrier = pltpu.get_barrier_semaphore()

    def tell(**where):
        pl.semaphore_signal(barrier, inc=1, device_id=where, device_id_type=MESH)

    partners = [lax.rem(head + d, nhead) for d in range(1, nhead)]
    for p in partners:
        tell(head=p)

    @pl.when(not_first)
    def _():
        tell(seq=prev_seq, sub=other, head=nhead - 1)

    @pl.when(upper)
    def _():
        tell(sub=0)

    @pl.when(fwd_in)
    def _():
        tell(sub=1)

    @pl.when(chain_in)
    def _():
        tell(seq=seq - 1)

    local = []
    for src, dst in ((x_ref.at[0, pl.ds(rows - 16, 16), :], x_last), (bc_ref.at[0, pl.ds(rows - 16, 16), :], bc_last),
                     (par_hbm, par_ref), (wx_hbm, wx_ref), (bx_hbm, bx_ref), (wb_hbm, wb_ref), (bb_hbm, bb_ref),
                     (gain_hbm, gain_ref)):
        local.append(pltpu.make_async_copy(src, dst, par_l.at[len(local)]))
    mine = pl.ds(pl.multiple_of(head * rows, rows), rows)
    local.append(pltpu.make_async_copy(dt_ref.at[0], dtf.at[mine, :], par_l.at[len(local)]))
    own = []
    for g in range(groups):
        at = pl.ds(pl.multiple_of(head * width + g * WIDE, WIDE), WIDE)
        bat = pl.ds(pl.multiple_of(head * bcw + g * 2 * STATE, 2 * STATE), 2 * STATE)
        own.append((pltpu.make_async_copy(x_ref.at[0, :, at], xf.at[g, mine, :], x_l.at[g]),
                    pltpu.make_async_copy(bc_ref.at[0, :, bat], bcf.at[g, mine, :], b_l.at[g])))
    for copy in local:
        copy.start()

    one = lambda cond: jnp.where(cond, 1, 0).astype(jnp.int32)
    peers = nhead - 1 + nhead * one(holds_tail) + one(lower) + one(chain_in) + one(chain_out)
    pl.semaphore_wait(barrier, peers)

    def remote(src, dst, send, recv, **where):
        return pltpu.make_async_remote_copy(
            src_ref=src, dst_ref=dst, send_sem=send, recv_sem=recv, device_id=where, device_id_type=MESH)

    def x_copy(d, g):
        at = pl.ds(pl.multiple_of(partners[d] * width + g * WIDE, WIDE), WIDE)
        return remote(x_ref.at[0, :, at], xf.at[g, mine, :], x_s.at[d, g], x_r.at[d, g], head=partners[d])

    def bc_copy(d, g):
        at = pl.ds(pl.multiple_of(partners[d] * bcw + g * 2 * STATE, 2 * STATE), 2 * STATE)
        return remote(bc_ref.at[0, :, at], bcf.at[g, mine, :], b_s.at[d, g], b_r.at[d, g], head=partners[d])

    def dt_copy(d):
        return remote(dt_ref.at[0], dtf.at[mine, :], d_s.at[d], d_r.at[d], head=partners[d])

    def tail_copy(k):
        return remote(tail_out.at[k], tail_in, t_s.at[k], t_r, seq=next_seq, sub=other, head=k)

    def end_copy():
        return remote(end_out, end_in, e_s, e_r, sub=other)

    def s_copy(g):
        return remote(sb.at[g], s0.at[g], s_s.at[g], s_r.at[g], sub=other)

    def chain_copy(g, i):
        at = pl.ds(i * PART, PART)
        return remote(eout.at[g, at], ein.at[g, at], c_s.at[g, i], c_r.at[g, i], seq=seq + 1)

    def fwd_copy(g, i):
        at = pl.ds(i * PART, PART)
        return remote(ein.at[g, at], ein.at[g, at], f_s.at[g, i], f_r.at[g, i], sub=other)

    for d in range(nhead - 1):
        dt_copy(d).start()
        bc_copy(d, 0).start()
        x_copy(d, 0).start()

    local[0].wait()
    local[1].wait()
    tail32[...] = jnp.zeros_like(tail32)
    for k in range(nhead):
        for j in range(groups):
            lo = k * width + j * WIDE
            tail32[3 * j:3 * j + 3, :] = x_last[:, lo:lo + WIDE].astype(F32)[13:16, :]
        lo = k * bcw
        tail32[12:15, 0:bcw] = bc_last[:, lo:lo + bcw].astype(F32)[13:16, :]
        tail_out[k] = tail32[...].astype(BF16)

    @pl.when(holds_tail)
    def _():
        for k in range(nhead):
            tail_copy(k).start()

    for g in range(1, groups):
        for d in range(nhead - 1):
            bc_copy(d, g).start()
            x_copy(d, g).start()

    for x_own, bc_own in own:
        bc_own.start()
        x_own.start()

    @pl.when(jnp.logical_not(not_first))
    def _():
        tail_in[...] = jnp.zeros_like(tail_in)

    @pl.when(seq == 0)
    def _():
        ein[...] = jnp.zeros_like(ein)

    for d in range(nhead - 1):
        dt_copy(d).wait_recv()
    for copy in local[2:]:
        copy.wait()
    dt_all = dtf[...].astype(F32)
    dt_own = dt_all
    for k in range(1, nhead):
        dt_own = jnp.where(head == k, pltpu.roll(dt_all, 128 - k * heads, 1), dt_own)
    par = par_ref[...]
    v = dt_own + par[0:1, :]
    u = jnp.exp(-jnp.abs(v))
    series = u * (1.0 - u * (0.5 - u * (1.0 / 3.0 - u * 0.25)))
    step = jnp.maximum(v, 0.0) + jnp.where(u < 0.03, series, jnp.log(1.0 + u))
    rate = -jnp.exp(par[1:2, :])
    row = lax.broadcasted_iota(jnp.int32, (SPAN, SPAN), 0)
    col = lax.broadcasted_iota(jnp.int32, (SPAN, SPAN), 1)
    causal = row >= col
    cum = jnp.dot(jnp.where(causal, 1.0, 0.0).astype(F32), rate * step,
                  preferred_element_type=F32, precision=lax.Precision.HIGHEST)
    cumt_sc[...] = jnp.transpose(cum)
    dtt_sc[...] = jnp.transpose(step)
    for g in range(groups):
        turn = (128 - g * PER_GROUP) % 128
        cum_g = pltpu.roll(cum, turn, 1) if turn else cum
        cum_sc[g] = cum_g
        dt_sc[g] = pltpu.roll(step, turn, 1) if turn else step
        par_sc[g] = pltpu.roll(par, turn, 1) if turn else par
        end_out[g] = jnp.broadcast_to(cum_g[SPAN - 1:SPAN, :], (8, 128))

    @pl.when(lower)
    def _():
        end_copy().start()

    @pl.when(upper)
    def _():
        end_copy().wait_recv()

    @pl.when(not_first)
    def _():
        tail_copy(0).wait_recv()

    tail32[...] = tail_in[...].astype(F32)
    left = col < HEAD_DIM

    def pair_wide(per_head, p):
        n = per_head.shape[0]
        a = jnp.broadcast_to(per_head[:, 2 * p:2 * p + 1], (n, 128))
        b = jnp.broadcast_to(per_head[:, 2 * p + 1:2 * p + 2], (n, 128))
        return jnp.where(left[0:n], a, b)

    def wide_row(per_head):
        return jnp.concatenate([pair_wide(per_head, p) for p in range(PAIRS)], axis=1)

    def conv(first, weights, bias, n):
        total = bias
        for k in range(4):
            total = total + weights[k:k + 1, :] * ext[5 + k:5 + k + SPAN, first:first + n]
        return (total * (1.0 / (1.0 + jnp.exp(-total)))).astype(BF16)

    lag = jnp.minimum(2 * seq + one(seq == 0), groups + 2)

    def chain(slot):
        g = slot - lag

        @pl.when(jnp.logical_and(upper, jnp.logical_and(g >= 0, g < groups)))
        def _():
            s_copy(g).wait_recv()
            d0 = jnp.exp(wide_row(end_in[g]))[0:1, :]
            d1 = jnp.exp(wide_row(end_out[g]))[0:1, :]
            for i in range(PARTS):
                at = slice(i * PART, (i + 1) * PART)

                @pl.when(chain_in)
                def _(i=i):
                    chain_copy(g, i).wait_recv()
                    fwd_copy(g, i).start()

                carried = d0 * ein[g, at, :].astype(F32) + s0[g, at, :].astype(F32)
                cb[g, at, :] = carried.astype(BF16)

                @pl.when(chain_out)
                def _(i=i, at=at, carried=carried):
                    eout[g, at, :] = (d1 * carried + st[g, at, :]).astype(BF16)
                    chain_copy(g, i).start()

    def within(g):
        inner = lax.dot_general(bcc[g, :, STATE:], bcc[g, :, 0:STATE], (((1,), (1,)), ((), ())),
                                preferred_element_type=F32)
        at = slice(g * PER_GROUP, (g + 1) * PER_GROUP)
        cum_rows, dt_rows = cumt_sc[at, :], dtt_sc[at, :]
        cum_g = cum_sc[g]
        skip = par_sc[g]
        for p in range(PAIRS):
            mix = []
            for j in (2 * p, 2 * p + 1):
                gap = jnp.broadcast_to(cum_g[:, j:j + 1], (SPAN, SPAN)) - cum_rows[j:j + 1, :]
                w = jnp.exp(jnp.where(causal, gap, -1e30)) * dt_rows[j:j + 1, :]
                mix.append((inner * w).astype(BF16))
            xp = xc[g, :, p * 128:(p + 1) * 128]
            y = jnp.dot(jnp.concatenate(mix, axis=0), xp, preferred_element_type=F32)
            y = jnp.where(left, y[0:SPAN], y[SPAN:])
            ysc[g, :, p * 128:(p + 1) * 128] = y + pair_wide(skip, p)[2:3, :] * xp.astype(F32)

    for g in range(groups):
        own[g][0].wait()
        own[g][1].wait()
        for d in range(nhead - 1):
            bc_copy(d, g).wait_recv()
            x_copy(d, g).wait_recv()
        lo = g * WIDE
        blo = g * 2 * STATE
        ext[8:8 + SPAN, 0:WIDE] = xf[g].astype(F32)
        ext[8:8 + SPAN, WIDE:WIDE + 2 * STATE] = bcf[g].astype(F32)
        ext[5:8, 0:WIDE] = tail32[3 * g:3 * g + 3, :]
        ext[5:8, WIDE:WIDE + 2 * STATE] = tail32[12:15, blo:blo + 2 * STATE]
        bcc[g] = conv(WIDE, wb_ref[:, blo:blo + 2 * STATE], bb_ref[:, blo:blo + 2 * STATE], 2 * STATE)
        b_in = bcc[g, :, 0:STATE]
        for p in range(PAIRS):
            q = p * 128
            xcp = conv(q, wx_ref[:, lo + q:lo + q + 128], bx_ref[:, lo + q:lo + q + 128], 128)
            xc[g, :, q:q + 128] = xcp
            cum_p = pair_wide(cum_sc[g], p)
            ecw[g, :, q:q + 128] = jnp.exp(cum_p)
            to_end = jnp.exp(cum_p[SPAN - 1:SPAN, :] - cum_p) * pair_wide(dt_sc[g], p)
            cb[g, :, q:q + 128] = (to_end * xcp.astype(F32)).astype(BF16)
        state = lax.dot_general(b_in, cb[g], (((0,), (0,)), ((), ())), preferred_element_type=F32)

        @pl.when(lower)
        def _(state=state, g=g):
            sb[g] = state.astype(BF16)
            s_copy(g).start()

        @pl.when(upper)
        def _(state=state, g=g):
            st[g] = state

        chain(g)
        if g > 0:
            within(g - 1)

    chain(groups)
    within(groups - 1)
    chain(groups + 1)

    def third(g, carry):
        chain(groups + 2 + g)

        @pl.when(lower)
        def _():
            @pl.when(fwd_in)
            def _():
                for i in range(PARTS):
                    fwd_copy(g, i).wait_recv()

            cb[g] = ein[g]

        y = jnp.dot(bcc[g, :, STATE:], cb[g], preferred_element_type=F32)
        y = y * ecw[g] + ysc[g]
        mean = jnp.mean(y * y, axis=1, keepdims=True)
        at = pl.ds(pl.multiple_of(g * WIDE, WIDE), WIDE)
        out_ref[0, :, at] = (y * lax.rsqrt(mean + NORM_EPSILON) * gain_ref[:, at]).astype(BF16)
        return carry

    lax.fori_loop(0, groups, third, 0)

    for d in range(nhead - 1):
        dt_copy(d).wait_send()
        for g in range(groups):
            bc_copy(d, g).wait_send()
            x_copy(d, g).wait_send()

    @pl.when(holds_tail)
    def _():
        for k in range(nhead):
            tail_copy(k).wait_send()

    @pl.when(lower)
    def _():
        end_copy().wait_send()
        for g in range(groups):
            s_copy(g).wait_send()

    @pl.when(chain_in)
    def _():
        for g in range(groups):
            for i in range(PARTS):
                fwd_copy(g, i).wait_send()

    @pl.when(chain_out)
    def _():
        for g in range(groups):
            for i in range(PARTS):
                chain_copy(g, i).wait_send()


def on_device(nseq, nhead, x_raw, bc_raw, dt_raw, conv_x_weight, conv_x_bias, conv_bc_weight, conv_bc_bias,
              stride_offset_per_head, a_log, skip_d, norm_gain):
    width = conv_x_weight.shape[1]
    groups = width // WIDE
    heads = a_log.shape[0]
    par = jnp.pad(jnp.stack([stride_offset_per_head, a_log, skip_d]), ((0, 5), (0, 128 - heads)))
    V = pltpu.VMEM
    dma = lambda *s: pltpu.SemaphoreType.DMA(s)
    g3 = (groups, STATE, WIDE)
    return pl.pallas_call(
        functools.partial(kernel, nseq, nhead),
        out_shape=jax.ShapeDtypeStruct((1, SPAN, width), BF16),
        in_specs=[pl.BlockSpec(memory_space=pltpu.HBM)] * 9,
        out_specs=pl.BlockSpec(memory_space=pltpu.VMEM),
        scratch_shapes=[
            V(conv_x_weight.shape, F32), V((1, width), F32), V(conv_bc_weight.shape, F32),
            V((1, conv_bc_weight.shape[1]), F32), V((8, 128), F32), V((1, width), F32),
            V((16, x_raw.shape[2]), BF16), V((16, bc_raw.shape[2]), BF16), dma(9), dma(groups), dma(groups),
            V(g3, BF16), V((groups, SPAN, 2 * STATE), BF16), V((SPAN, 128), BF16),
            V(g3, BF16), V((groups, SPAN, 2 * STATE), BF16), V((SPAN + 8, WIDE + 2 * STATE), F32),
            V((16, WIDE), F32), V((nhead, 16, WIDE), BF16), V((16, WIDE), BF16),
            V((groups, SPAN, 128), F32), V((groups, SPAN, 128), F32), V((128, SPAN), F32), V((128, SPAN), F32),
            V((groups, 8, 128), F32), V((groups, 8, 128), F32), V((groups, 8, 128), F32),
            V(g3, F32), V(g3, BF16), V(g3, BF16), V(g3, BF16), V(g3, BF16), V(g3, BF16), V(g3, F32), V(g3, F32),
            dma(nhead - 1, groups), dma(nhead - 1, groups), dma(nhead - 1, groups), dma(nhead - 1, groups),
            dma(nhead - 1), dma(nhead - 1), dma(nhead), pltpu.SemaphoreType.DMA,
            pltpu.SemaphoreType.DMA, pltpu.SemaphoreType.DMA, dma(groups), dma(groups),
            dma(groups, PARTS), dma(groups, PARTS), dma(groups, PARTS), dma(groups, PARTS),
        ],
        compiler_params=pltpu.CompilerParams(
            collective_id=0, has_side_effects=True, vmem_limit_bytes=64 * 1024 * 1024 - 131072),
    )(x_raw, bc_raw, dt_raw, conv_x_weight, conv_x_bias[None], conv_bc_weight, conv_bc_bias[None], par,
      norm_gain[None])


def solution(mesh):
    placed = (
        P(("groups", "seq", "sub"), "head", None),
        P(("groups", "seq", "sub"), "head", None),
        P(("groups", "seq", "sub"), "head", None),
        P(None, "head"),
        P("head"),
        P(None, "head"),
        P("head"),
        P("head"),
        P("head"),
        P("head"),
        P("head"),
    )
    return jax.shard_map(
        functools.partial(on_device, mesh.shape["seq"], mesh.shape["head"]),
        mesh=mesh,
        in_specs=placed,
        out_specs=P(("groups", "seq", "sub"), None, "head"),
        check_vma=False,
    )
```

```python
import functools
import jax
import jax.numpy as jnp
from jax import lax
from jax.experimental import pallas as pl
from jax.experimental.pallas import tpu as pltpu
from jax.sharding import PartitionSpec as P

STATE = 128
SPAN = 128
HEAD_DIM = 64
PER_GROUP = 16
WIDE = PER_GROUP * HEAD_DIM
PAIRS = PER_GROUP // 2
NORM_EPSILON = 1e-05
PARTS = 4
PART = STATE // PARTS
MESH = pl.DeviceIdType.MESH
F32 = jnp.float32
BF16 = jnp.bfloat16


def kernel(nseq, nhead, x_ref, bc_ref, dt_ref, wx_hbm, bx_hbm, wb_hbm, bb_hbm, par_hbm, gain_hbm, out_ref,
           wx_ref, bx_ref, wb_ref, bb_ref, par_ref, gain_ref, x_last, bc_last, par_l, x_l, b_l, outv, o_l,
           xf, bcf, dtf, xc, bcc, ext, tail32, tail_out, tail_in, cum_sc, dt_sc, cumt_sc, dtt_sc, par_sc,
           end_out, end_in, st, sb, s0, ein, eout, cb, ysc, ecw,
           x_s, x_r, b_s, b_r, d_s, d_r, t_s, t_r, e_s, e_r, s_s, s_r, c_s, c_r, f_s, f_r):
    seq = lax.axis_index("seq")
    head = lax.axis_index("head")
    sub = lax.axis_index("sub")
    rows = x_ref.shape[1]
    groups = xf.shape[0]
    width = groups * WIDE
    bcw = groups * 2 * STATE
    heads = groups * PER_GROUP
    not_first = jnp.logical_or(seq > 0, sub > 0)
    not_last = jnp.logical_or(seq < nseq - 1, sub < 1)
    holds_tail = jnp.logical_and(not_last, head == nhead - 1)
    next_seq, prev_seq = seq + sub, seq + sub - 1
    other = 1 - sub
    lower, upper = sub == 0, sub == 1
    chain_in = jnp.logical_and(upper, seq > 0)
    chain_out = jnp.logical_and(upper, seq < nseq - 1)
    fwd_in = jnp.logical_and(lower, seq > 0)

    barrier = pltpu.get_barrier_semaphore()

    def tell(**where):
        pl.semaphore_signal(barrier, inc=1, device_id=where, device_id_type=MESH)

    partners = [lax.rem(head + d, nhead) for d in range(1, nhead)]
    for p in partners:
        tell(head=p)

    @pl.when(not_first)
    def _():
        tell(seq=prev_seq, sub=other, head=nhead - 1)

    @pl.when(upper)
    def _():
        tell(sub=0)

    @pl.when(fwd_in)
    def _():
        tell(sub=1)

    @pl.when(chain_in)
    def _():
        tell(seq=seq - 1)

    local = []
    for src, dst in ((x_ref.at[0, pl.ds(rows - 16, 16), :], x_last), (bc_ref.at[0, pl.ds(rows - 16, 16), :], bc_last),
                     (par_hbm, par_ref), (wx_hbm, wx_ref), (bx_hbm, bx_ref), (wb_hbm, wb_ref), (bb_hbm, bb_ref),
                     (gain_hbm, gain_ref)):
        local.append(pltpu.make_async_copy(src, dst, par_l.at[len(local)]))
    mine = pl.ds(pl.multiple_of(head * rows, rows), rows)
    local.append(pltpu.make_async_copy(dt_ref.at[0], dtf.at[mine, :], par_l.at[len(local)]))
    own = []
    for g in range(groups):
        at = pl.ds(pl.multiple_of(head * width + g * WIDE, WIDE), WIDE)
        bat = pl.ds(pl.multiple_of(head * bcw + g * 2 * STATE, 2 * STATE), 2 * STATE)
        own.append((pltpu.make_async_copy(x_ref.at[0, :, at], xf.at[g, mine, :], x_l.at[g]),
                    pltpu.make_async_copy(bc_ref.at[0, :, bat], bcf.at[g, mine, :], b_l.at[g])))
    for copy in local:
        copy.start()

    one = lambda cond: jnp.where(cond, 1, 0).astype(jnp.int32)
    peers = nhead - 1 + nhead * one(holds_tail) + one(lower) + one(chain_in) + one(chain_out)
    pl.semaphore_wait(barrier, peers)

    def remote(src, dst, send, recv, **where):
        return pltpu.make_async_remote_copy(
            src_ref=src, dst_ref=dst, send_sem=send, recv_sem=recv, device_id=where, device_id_type=MESH)

    def x_copy(d, g):
        at = pl.ds(pl.multiple_of(partners[d] * width + g * WIDE, WIDE), WIDE)
        return remote(x_ref.at[0, :, at], xf.at[g, mine, :], x_s.at[d, g], x_r.at[d, g], head=partners[d])

    def bc_copy(d, g):
        at = pl.ds(pl.multiple_of(partners[d] * bcw + g * 2 * STATE, 2 * STATE), 2 * STATE)
        return remote(bc_ref.at[0, :, at], bcf.at[g, mine, :], b_s.at[d, g], b_r.at[d, g], head=partners[d])

    def dt_copy(d):
        return remote(dt_ref.at[0], dtf.at[mine, :], d_s.at[d], d_r.at[d], head=partners[d])

    def tail_copy(k):
        return remote(tail_out.at[k], tail_in, t_s.at[k], t_r, seq=next_seq, sub=other, head=k)

    def end_copy():
        return remote(end_out, end_in, e_s, e_r, sub=other)

    def s_copy(g):
        return remote(sb.at[g], s0.at[g], s_s.at[g], s_r.at[g], sub=other)

    def chain_copy(g, i):
        at = pl.ds(i * PART, PART)
        return remote(eout.at[g, at], ein.at[g, at], c_s.at[g, i], c_r.at[g, i], seq=seq + 1)

    def fwd_copy(g, i):
        at = pl.ds(i * PART, PART)
        return remote(ein.at[g, at], ein.at[g, at], f_s.at[g, i], f_r.at[g, i], sub=other)

    for d in range(nhead - 1):
        dt_copy(d).start()
        bc_copy(d, 0).start()
        x_copy(d, 0).start()

    local[0].wait()
    local[1].wait()
    tail32[...] = jnp.zeros_like(tail32)
    for k in range(nhead):
        for j in range(groups):
            lo = k * width + j * WIDE
            tail32[3 * j:3 * j + 3, :] = x_last[:, lo:lo + WIDE].astype(F32)[13:16, :]
        lo = k * bcw
        tail32[12:15, 0:bcw] = bc_last[:, lo:lo + bcw].astype(F32)[13:16, :]
        tail_out[k] = tail32[...].astype(BF16)

    @pl.when(holds_tail)
    def _():
        for k in range(nhead):
            tail_copy(k).start()

    for g in range(1, groups):
        for d in range(nhead - 1):
            bc_copy(d, g).start()
            x_copy(d, g).start()

    for x_own, bc_own in own:
        bc_own.start()
        x_own.start()

    @pl.when(jnp.logical_not(not_first))
    def _():
        tail_in[...] = jnp.zeros_like(tail_in)

    @pl.when(seq == 0)
    def _():
        ein[...] = jnp.zeros_like(ein)

    for d in range(nhead - 1):
        dt_copy(d).wait_recv()
    for copy in local[2:]:
        copy.wait()
    dt_all = dtf[...].astype(F32)
    dt_own = dt_all
    for k in range(1, nhead):
        dt_own = jnp.where(head == k, pltpu.roll(dt_all, 128 - k * heads, 1), dt_own)
    par = par_ref[...]
    v = dt_own + par[0:1, :]
    u = jnp.exp(-jnp.abs(v))
    series = u * (1.0 - u * (0.5 - u * (1.0 / 3.0 - u * 0.25)))
    step = jnp.maximum(v, 0.0) + jnp.where(u < 0.03, series, jnp.log(1.0 + u))
    rate = -jnp.exp(par[1:2, :])
    row = lax.broadcasted_iota(jnp.int32, (SPAN, SPAN), 0)
    col = lax.broadcasted_iota(jnp.int32, (SPAN, SPAN), 1)
    causal = row >= col
    cum = jnp.dot(jnp.where(causal, 1.0, 0.0).astype(F32), rate * step,
                  preferred_element_type=F32, precision=lax.Precision.HIGHEST)
    cumt_sc[...] = jnp.transpose(cum)
    dtt_sc[...] = jnp.transpose(step)
    for g in range(groups):
        turn = (128 - g * PER_GROUP) % 128
        cum_g = pltpu.roll(cum, turn, 1) if turn else cum
        cum_sc[g] = cum_g
        dt_sc[g] = pltpu.roll(step, turn, 1) if turn else step
        par_sc[g] = pltpu.roll(par, turn, 1) if turn else par
        end_out[g] = jnp.broadcast_to(cum_g[SPAN - 1:SPAN, :], (8, 128))

    @pl.when(lower)
    def _():
        end_copy().start()

    @pl.when(upper)
    def _():
        end_copy().wait_recv()

    @pl.when(not_first)
    def _():
        tail_copy(0).wait_recv()

    tail32[...] = tail_in[...].astype(F32)
    left = col < HEAD_DIM

    def pair_wide(per_head, p):
        n = per_head.shape[0]
        a = jnp.broadcast_to(per_head[:, 2 * p:2 * p + 1], (n, 128))
        b = jnp.broadcast_to(per_head[:, 2 * p + 1:2 * p + 2], (n, 128))
        return jnp.where(left[0:n], a, b)

    def wide_row(per_head):
        return jnp.concatenate([pair_wide(per_head, p) for p in range(PAIRS)], axis=1)

    def conv(first, weights, bias, n):
        total = bias
        for k in range(4):
            total = total + weights[k:k + 1, :] * ext[5 + k:5 + k + SPAN, first:first + n]
        return (total * (1.0 / (1.0 + jnp.exp(-total)))).astype(BF16)

    lag = jnp.minimum(2 * seq + one(seq == 0), groups + 2)

    def chain(slot):
        g = slot - lag

        @pl.when(jnp.logical_and(upper, jnp.logical_and(g >= 0, g < groups)))
        def _():
            s_copy(g).wait_recv()
            d0 = jnp.exp(wide_row(end_in[g]))[0:1, :]
            d1 = jnp.exp(wide_row(end_out[g]))[0:1, :]
            for i in range(PARTS):
                at = slice(i * PART, (i + 1) * PART)

                @pl.when(chain_in)
                def _(i=i):
                    chain_copy(g, i).wait_recv()
                    fwd_copy(g, i).start()

                carried = d0 * ein[g, at, :].astype(F32) + s0[g, at, :].astype(F32)
                cb[g, at, :] = carried.astype(BF16)

                @pl.when(chain_out)
                def _(i=i, at=at, carried=carried):
                    eout[g, at, :] = (d1 * carried + st[g, at, :]).astype(BF16)
                    chain_copy(g, i).start()

    def within(g):
        inner = lax.dot_general(bcc[g, :, STATE:], bcc[g, :, 0:STATE], (((1,), (1,)), ((), ())),
                                preferred_element_type=F32)
        at = slice(g * PER_GROUP, (g + 1) * PER_GROUP)
        cum_rows, dt_rows = cumt_sc[at, :], dtt_sc[at, :]
        cum_g = cum_sc[g]
        skip = par_sc[g]
        for p in range(PAIRS):
            mix = []
            for j in (2 * p, 2 * p + 1):
                gap = jnp.broadcast_to(cum_g[:, j:j + 1], (SPAN, SPAN)) - cum_rows[j:j + 1, :]
                w = jnp.exp(jnp.where(causal, gap, -1e30)) * dt_rows[j:j + 1, :]
                mix.append((inner * w).astype(BF16))
            xp = xc[g, :, p * 128:(p + 1) * 128]
            y = jnp.dot(jnp.concatenate(mix, axis=0), xp, preferred_element_type=F32)
            y = jnp.where(left, y[0:SPAN], y[SPAN:])
            ysc[g, :, p * 128:(p + 1) * 128] = y + pair_wide(skip, p)[2:3, :] * xp.astype(F32)

    for g in range(groups):
        own[g][0].wait()
        own[g][1].wait()
        for d in range(nhead - 1):
            bc_copy(d, g).wait_recv()
            x_copy(d, g).wait_recv()
        lo = g * WIDE
        blo = g * 2 * STATE
        ext[8:8 + SPAN, 0:WIDE] = xf[g].astype(F32)
        ext[8:8 + SPAN, WIDE:WIDE + 2 * STATE] = bcf[g].astype(F32)
        ext[5:8, 0:WIDE] = tail32[3 * g:3 * g + 3, :]
        ext[5:8, WIDE:WIDE + 2 * STATE] = tail32[12:15, blo:blo + 2 * STATE]
        bcc[g] = conv(WIDE, wb_ref[:, blo:blo + 2 * STATE], bb_ref[:, blo:blo + 2 * STATE], 2 * STATE)
        b_in = bcc[g, :, 0:STATE]
        for p in range(PAIRS):
            q = p * 128
            xcp = conv(q, wx_ref[:, lo + q:lo + q + 128], bx_ref[:, lo + q:lo + q + 128], 128)
            xc[g, :, q:q + 128] = xcp
            cum_p = pair_wide(cum_sc[g], p)
            ecw[g, :, q:q + 128] = jnp.exp(cum_p)
            to_end = jnp.exp(cum_p[SPAN - 1:SPAN, :] - cum_p) * pair_wide(dt_sc[g], p)
            cb[g, :, q:q + 128] = (to_end * xcp.astype(F32)).astype(BF16)
        state = lax.dot_general(b_in, cb[g], (((0,), (0,)), ((), ())), preferred_element_type=F32)

        @pl.when(lower)
        def _(state=state, g=g):
            sb[g] = state.astype(BF16)
            s_copy(g).start()

        @pl.when(upper)
        def _(state=state, g=g):
            st[g] = state

        chain(g)
        if g > 0:
            within(g - 1)

    chain(groups)
    within(groups - 1)
    chain(groups + 1)

    def out_copy(g):
        at = pl.ds(pl.multiple_of(g * WIDE, WIDE), WIDE)
        return pltpu.make_async_copy(outv.at[g], out_ref.at[0, :, at], o_l.at[g])

    def third(g, carry):
        chain(groups + 2 + g)

        @pl.when(lower)
        def _():
            @pl.when(fwd_in)
            def _():
                for i in range(PARTS):
                    fwd_copy(g, i).wait_recv()

            cb[g] = ein[g]

        y = jnp.dot(bcc[g, :, STATE:], cb[g], preferred_element_type=F32)
        y = y * ecw[g] + ysc[g]
        mean = jnp.mean(y * y, axis=1, keepdims=True)
        at = pl.ds(pl.multiple_of(g * WIDE, WIDE), WIDE)
        outv[g] = (y * lax.rsqrt(mean + NORM_EPSILON) * gain_ref[:, at]).astype(BF16)
        out_copy(g).start()
        return carry

    lax.fori_loop(0, groups, third, 0)
    for g in range(groups):
        out_copy(g).wait()

    for d in range(nhead - 1):
        dt_copy(d).wait_send()
        for g in range(groups):
            bc_copy(d, g).wait_send()
            x_copy(d, g).wait_send()

    @pl.when(holds_tail)
    def _():
        for k in range(nhead):
            tail_copy(k).wait_send()

    @pl.when(lower)
    def _():
        end_copy().wait_send()
        for g in range(groups):
            s_copy(g).wait_send()

    @pl.when(chain_in)
    def _():
        for g in range(groups):
            for i in range(PARTS):
                fwd_copy(g, i).wait_send()

    @pl.when(chain_out)
    def _():
        for g in range(groups):
            for i in range(PARTS):
                chain_copy(g, i).wait_send()


def on_device(nseq, nhead, x_raw, bc_raw, dt_raw, conv_x_weight, conv_x_bias, conv_bc_weight, conv_bc_bias,
              stride_offset_per_head, a_log, skip_d, norm_gain):
    width = conv_x_weight.shape[1]
    groups = width // WIDE
    heads = a_log.shape[0]
    par = jnp.pad(jnp.stack([stride_offset_per_head, a_log, skip_d]), ((0, 5), (0, 128 - heads)))
    V = pltpu.VMEM
    dma = lambda *s: pltpu.SemaphoreType.DMA(s)
    g3 = (groups, STATE, WIDE)
    return pl.pallas_call(
        functools.partial(kernel, nseq, nhead),
        out_shape=jax.ShapeDtypeStruct((1, SPAN, width), BF16),
        in_specs=[pl.BlockSpec(memory_space=pltpu.HBM)] * 9,
        out_specs=pl.BlockSpec(memory_space=pltpu.HBM),
        scratch_shapes=[
            V(conv_x_weight.shape, F32), V((1, width), F32), V(conv_bc_weight.shape, F32),
            V((1, conv_bc_weight.shape[1]), F32), V((8, 128), F32), V((1, width), F32),
            V((16, x_raw.shape[2]), BF16), V((16, bc_raw.shape[2]), BF16), dma(9), dma(groups), dma(groups), V(g3, BF16), dma(groups),
            V(g3, BF16), V((groups, SPAN, 2 * STATE), BF16), V((SPAN, 128), BF16),
            V(g3, BF16), V((groups, SPAN, 2 * STATE), BF16), V((SPAN + 8, WIDE + 2 * STATE), F32),
            V((16, WIDE), F32), V((nhead, 16, WIDE), BF16), V((16, WIDE), BF16),
            V((groups, SPAN, 128), F32), V((groups, SPAN, 128), F32), V((128, SPAN), F32), V((128, SPAN), F32),
            V((groups, 8, 128), F32), V((groups, 8, 128), F32), V((groups, 8, 128), F32),
            V(g3, F32), V(g3, BF16), V(g3, BF16), V(g3, BF16), V(g3, BF16), V(g3, BF16), V(g3, F32), V(g3, F32),
            dma(nhead - 1, groups), dma(nhead - 1, groups), dma(nhead - 1, groups), dma(nhead - 1, groups),
            dma(nhead - 1), dma(nhead - 1), dma(nhead), pltpu.SemaphoreType.DMA,
            pltpu.SemaphoreType.DMA, pltpu.SemaphoreType.DMA, dma(groups), dma(groups),
            dma(groups, PARTS), dma(groups, PARTS), dma(groups, PARTS), dma(groups, PARTS),
        ],
        compiler_params=pltpu.CompilerParams(
            collective_id=0, has_side_effects=True, vmem_limit_bytes=64 * 1024 * 1024 - 131072),
    )(x_raw, bc_raw, dt_raw, conv_x_weight, conv_x_bias[None], conv_bc_weight, conv_bc_bias[None], par,
      norm_gain[None])


def solution(mesh):
    placed = (
        P(("groups", "seq", "sub"), "head", None),
        P(("groups", "seq", "sub"), "head", None),
        P(("groups", "seq", "sub"), "head", None),
        P(None, "head"),
        P("head"),
        P(None, "head"),
        P("head"),
        P("head"),
        P("head"),
        P("head"),
        P("head"),
    )
    return jax.shard_map(
        functools.partial(on_device, mesh.shape["seq"], mesh.shape["head"]),
        mesh=mesh,
        in_specs=placed,
        out_specs=P(("groups", "seq", "sub"), None, "head"),
        check_vma=False,
    )
```
